128 devices in a mesh: row: 8 (over z_lo, x), col: 16 (over y, z_hi, core).
Axes of the slice: x: 4, y: 4, z: 4 (z_hi: 2, z_lo: 2; z = z_hi * 2 + z_lo), core: 2. Of those that a mesh axis runs over, the one named last changes fastest.
Arguments:
- amplitudes: float32 [2048, 16384], P('col', 'row'), may hold values from -6 to 6
- integrals: float32 [16384, 16384], P('row', 'col'), as said below
- amp_mask: int32 [16, 128], replicated, may hold values 0 or 1
- int_mask: int32 [128, 128], replicated, may hold values 0 or 1
- pairs: int32 [2048, 2], P('row'), may hold values from 0 to 199, as said below
- eps_occ: float32 [200], replicated, may hold values from -2 to -0.3
- eps_vir: float32 [128], replicated, may hold values from 0.3 to 3
Outputs:
- update: float32 [2048, 16384], P('row', 'col')
The draws below stay inside these ranges and needn't reach their ends.
Inputs may be any that keep to these rules, and one draw needn't show every extreme that they name: `pairs`: rows p and p + 1024 name the same two occupied orbitals in swapped order; the first half holds every pair of 16 distinct orbitals with 64 other distinct orbitals. integrals[c * 128 + d, a * 128 + b] equals integrals[d * 128 + c, b * 128 + a] exactly.
All inputs are finite; a program needn't handle non-finite values.
Results may differ from the reference program's by a relative error of at most 0.000071.
Values sent between devices are 32-bit elements; how exact they have to be, the bound alone decides.
A program may use at most 128 MiB of HBM per device.

```python
import math
import jax
import jax.numpy as jnp
from jax import lax

NO = 200
VW = 128
TILE = 128
OI = 16
OJ = 64
VP = 16384
P_SIZE = 2048
PT = 16


def draw_pairs(key, part):
    key = jax.random.fold_in(key, 11)
    order = jax.random.permutation(key, NO).astype(jnp.int32)
    first = order[:OI]
    second = order[OI:OI + OJ]
    left = jnp.repeat(first, OJ)
    right = jnp.tile(second, OI)
    upper = jnp.stack([left, right], axis=1)
    lower = jnp.stack([right, left], axis=1)
    return jnp.concatenate([upper, lower], axis=0).astype(jnp.int32)


def draw_integrals(key, part):
    key = jax.random.fold_in(key, 23)
    shape = (VW, VW, VW, VW)
    base = jax.random.normal(key, shape, jnp.float32)
    both = base + jnp.transpose(base, (1, 0, 3, 2))
    return (both * (2.0 * VW * VW) ** (-0.5)).reshape(VW * VW, VW * VW)


def plant(drawn, rng, low, largest):
    longest = drawn.shape.index(max(drawn.shape))
    spots = []
    for shift in (0, 1):
        where = [jax.random.randint(jax.random.fold_in(rng, axis), (), 0, length) for axis, length in enumerate(drawn.shape)]
        where[longest] = (where[longest] + shift) % drawn.shape[longest]
        spots.append(tuple(where))
    return drawn.at[spots[0]].set(low).at[spots[1]].set(largest)


def block_levels(rng, dims, cuts, low, top_value):
    gain, own = 1.0, jax.random.fold_in(rng, 6)
    for axis_at, parts in cuts:
        heights = jnp.exp(jax.random.uniform(jax.random.fold_in(own, axis_at), (parts,), jnp.float32, low / len(cuts), top_value / len(cuts)))
        gain = gain * jnp.repeat(heights, dims[axis_at] // parts).reshape([-1 if axis == axis_at else 1 for axis in range(len(dims))])
    return gain


def bell_draw(own_key, extent, width, reach, cuts=(), kind=jnp.bfloat16):
    result = jax.random.normal(own_key, extent, jnp.float32) * width
    if len(cuts) > 0:
        result = block_levels(own_key, extent, cuts, -0.22, 0.18) * result
    return jnp.clip(result, min=-reach, max=reach).astype(kind)


def setup_inputs(seed: int = 0) -> dict:
    key_list = jax.random.split(jax.random.key(seed), 8)
    return {
        "amplitudes": bell_draw(key_list[0], (P_SIZE, VP), 1.0, 6.0, ((0, 16), (1, 8)), jnp.float32),
        "integrals": draw_integrals(jax.random.fold_in(key_list[7], 71), 0),
        "amp_mask": plant((jax.random.randint(key_list[2], (PT, VW), 0, 3) < 2).astype(jnp.int32), jax.random.fold_in(key_list[2], 1), 0, 1),
        "int_mask": plant((jax.random.randint(key_list[3], (VW, VW), 0, 4) < 3).astype(jnp.int32), jax.random.fold_in(key_list[3], 1), 0, 1),
        "pairs": draw_pairs(jax.random.fold_in(key_list[7], 71), 0),
        "eps_occ": jnp.clip(jax.random.uniform(key_list[5], (NO,), jnp.float32, -2.0, -0.3), -2.0, -0.3),
        "eps_vir": jnp.clip(jnp.exp(jax.random.uniform(key_list[6], (VW,), jnp.float32, math.log(0.3), math.log(3.0))), 0.3, 3.0),
    }


def reference(amplitudes, integrals, amp_mask, int_mask, pairs, eps_occ, eps_vir):
    count = amplitudes.shape[0]
    tile_mask = jnp.repeat(jnp.repeat(amp_mask.astype(jnp.float32), TILE, axis=0), VW, axis=1)
    masked_t = amplitudes * tile_mask
    coupling = int_mask.astype(jnp.float32)
    pair_mask = (coupling[:, None, :, None] * coupling[None, :, None, :]).reshape(VP, VP)
    masked_v = integrals * pair_mask
    ladder = jnp.dot(masked_t, masked_v, precision=lax.Precision.HIGHEST, preferred_element_type=jnp.float32)
    half = count // 2
    swapped = jnp.concatenate([ladder[half:], ladder[:half]], axis=0)
    mirrored = jnp.transpose(swapped.reshape(count, VW, VW), (0, 2, 1)).reshape(count, VP)
    occ_energy = eps_occ[pairs[:, 0]] + eps_occ[pairs[:, 1]]
    vir_energy = (eps_vir[:, None] + eps_vir[None, :]).reshape(VP)
    denom = vir_energy[None, :] - occ_energy[:, None]
    return (ladder + mirrored) / denom
```

```python
import functools

import jax
import jax.numpy as jnp
from jax import lax
from jax.experimental import pallas as pl
from jax.experimental.pallas import tpu as pltpu
from jax.sharding import PartitionSpec as P

MESH = pl.DeviceIdType.MESH
ROUNDS = 4
ROWS = 64 // ROUNDS
HALF = ROWS // 2
F32 = jnp.float32
BF16 = jnp.bfloat16


def swap_bits(tiles, tile_bit, lane_bit):
    step = 1 << lane_bit
    lane = lax.broadcasted_iota(jnp.int32, tiles[0].shape, len(tiles[0].shape) - 1)
    upper = (lane & step) != 0
    result = list(tiles)
    for low in range(len(tiles)):
        if low >> tile_bit & 1:
            continue
        high = low | 1 << tile_bit
        a, b = tiles[low], tiles[high]
        result[low] = jnp.where(upper, pltpu.roll(b, step, 1), a)
        result[high] = jnp.where(upper, b, pltpu.roll(a, 128 - step, 1))
    return result


def split(value):
    hi = value.astype(BF16)
    return hi, (value - hi.astype(F32)).astype(BF16)


def kernel(
    t_hbm, v_hbm, am_s, im_s, im_v, pairs_v, eocc_v, evir_v, evir_s,
    out,
    tbuf, vbuf, vhi, vlo, pre_s, pre_r, slab, shi, slo, part, xr, zb, zr, post_s, post_r, occ, imf,
    load_sem, pre_ss, pre_rs, g_ss, g_rs, c_ss, c_rs, x_ss, x_rs, z_ss, z_rs, o_ss, o_rs,
):
    row = lax.axis_index("row")
    col = lax.axis_index("col")
    zlo, x = row // 4, lax.rem(row, 4)
    y, zhi, core = col // 4, lax.rem(col // 2, 2), lax.rem(col, 2)
    chip = col // 2
    row_z = lax.rem(row + 4, 8)
    col_far = lax.rem(col + 8, 16)
    up = lax.rem(y + 1, 4)
    down = lax.rem(y + 3, 4)
    opposite = lax.rem(y + 2, 4)
    flip = 1 - zhi

    def col_of(yy, zz):
        return yy * 4 + zz * 2 + core

    dev_up = (row, col_of(up, zhi))
    dev_down = (row, col_of(down, zhi))
    dev_z = (row, col_of(y, flip))
    dev_core = (row, chip * 2 + 1 - core)
    dev_zlo = (row_z, col)
    own_off = 64 * (y // 2)
    send_off = 64 - own_off

    barrier = pltpu.get_barrier_semaphore()
    peers = [(r, col_far) for r in range(8)]
    peers += [dev_up, dev_down, dev_z, dev_core]
    peers += [(zlo * 4 + lax.rem(x + dx, 4), col) for dx in (1, 2, 3)]
    peers += [(row_z, lax.rem(col + j, 16)) for j in range(16) if j != 8]
    for peer in peers:
        pl.semaphore_signal(barrier, inc=1, device_id=peer, device_id_type=MESH)

    t_load = pltpu.make_async_copy(t_hbm, tbuf, load_sem.at[16])
    t_load.start()

    def v_load(block):
        rows = pl.ds(block * 128, 128)
        return pltpu.make_async_copy(v_hbm.at[rows], vbuf.at[rows], load_sem.at[block])

    for block in range(16):
        v_load(block).start()

    def remote(src, dst, send_sem, recv_sem, device):
        return pltpu.make_async_remote_copy(
            src_ref=src, dst_ref=dst, send_sem=send_sem, recv_sem=recv_sem,
            device_id=device, device_id_type=MESH,
        )

    def drain(ref, sem):
        pltpu.make_async_copy(ref, ref, sem).wait()

    imf[...] = im_v[...].astype(F32)

    ids = lax.broadcasted_iota(jnp.int32, (256, 200), 1)
    first = jnp.sum(jnp.where(pairs_v[:, 0:1] == ids, eocc_v[...], 0.0), axis=1, keepdims=True)
    second = jnp.sum(jnp.where(pairs_v[:, 1:2] == ids, eocc_v[...], 0.0), axis=1, keepdims=True)
    occ[...] = jnp.broadcast_to(first + second, (256, 128))

    t_load.wait()

    def masked_tile(offset, q, j):
        rows = pl.ds(pl.multiple_of(offset + q * ROWS, 8), ROWS)
        return tbuf[rows, j * 128 : (j + 1) * 128] * am_s[col, row * 16 + j].astype(F32)

    def pre_shuffle(q):
        tiles = [masked_tile(send_off, q, j) for j in range(16)]
        for bit in range(4):
            tiles = swap_bits(tiles, bit, bit)
        for bit in range(3):
            tiles = swap_bits(tiles, bit, bit + 4)
        for j in range(16):
            pre_s[q, j % 8, j // 8] = tiles[j]

    def pre_send(q):
        for r in range(8):
            remote(
                pre_s.at[q, r], pre_r.at[q, row], pre_ss.at[q], pre_rs.at[q], (r, col_far)
            ).start()

    pre_shuffle(0)
    pl.semaphore_wait(barrier, len(peers))
    pre_send(0)
    pre_shuffle(1)
    pre_send(1)
    for q in range(2, ROUNDS):
        pre_shuffle(q)

    def convert(block, _):
        v_load(block).wait()
        rows = pl.ds(pl.multiple_of(block * 128, 128), 128)
        for al in range(8):
            lanes = slice(al * 128, (al + 1) * 128)
            weight = im_s[row * 16 + block, col * 8 + al].astype(F32)
            hi, lo = split(vbuf[rows, lanes] * imf[...] * weight)
            vhi[rows, lanes] = hi
            vlo[rows, lanes] = lo
        return 0

    def slot(q, yy, zz, rows=None):
        ref = slab.at[q, core, yy * 2 + zz]
        return ref if rows is None else ref.at[rows]

    LOWER, UPPER = pl.ds(0, HALF), pl.ds(HALF, HALF)

    def push(q, kind, yy, zz, device, rows=None):
        ref = slot(q, yy, zz, rows)
        remote(ref, ref, g_ss.at[q], g_rs.at[q, kind], device).start()

    def arrived(q, kind, yy, zz, rows=None):
        drain(slot(q, yy, zz, rows), g_rs.at[q, kind])

    def to_core(q, yy, zz):
        ref = slot(q, yy, zz)
        remote(ref, ref, c_ss.at[q], c_rs.at[q], dev_core).start()

    def g1(q):
        drain(pre_r.at[q], pre_rs.at[q])
        tiles = [pre_r[q, j % 8, j // 8] for j in range(16)]
        for bit in range(3):
            tiles = swap_bits(tiles, bit, bit + 4)
        for j in range(16):
            slab[q, core, chip, :, j * 128 : (j + 1) * 128] = masked_tile(own_off, q, j) + tiles[j]
        push(q, 0, y, zhi, dev_z)
        push(q, 1, y, zhi, dev_up)
        push(q, 2, y, zhi, dev_down)
        to_core(q, y, zhi)

    def g2(q):
        arrived(q, 1, down, zhi)
        push(q, 3, down, zhi, dev_up, LOWER)
        to_core(q, down, zhi)
        arrived(q, 2, up, zhi)
        push(q, 4, up, zhi, dev_down, UPPER)
        to_core(q, up, zhi)
        arrived(q, 0, y, flip)
        push(q, 5, y, flip, dev_up)
        push(q, 6, y, flip, dev_down)
        to_core(q, y, flip)

    def g3(q):
        arrived(q, 3, opposite, zhi, LOWER)
        arrived(q, 4, opposite, zhi, UPPER)
        to_core(q, opposite, zhi)
        arrived(q, 5, down, flip)
        push(q, 7, down, flip, dev_up, LOWER)
        to_core(q, down, flip)
        arrived(q, 6, up, flip)
        push(q, 8, up, flip, dev_down, UPPER)
        to_core(q, up, flip)

    def g4(q):
        arrived(q, 7, opposite, flip, LOWER)
        arrived(q, 8, opposite, flip, UPPER)
        to_core(q, opposite, flip)

    def mm(q):
        drain(slab.at[q, 0], c_rs.at[q])
        for k in range(2):
            for c in range(8):
                rows = slice((k * 8 + c) * ROWS, (k * 8 + c + 1) * ROWS)
                hi, lo = split(slab[q, k, c])
                shi[rows, :] = hi
                slo[rows, :] = lo

        def tile(n, _):
            lanes = pl.ds(pl.multiple_of(n * 256, 256), 256)
            dot = functools.partial(jnp.dot, preferred_element_type=F32)
            acc = dot(shi[...], vhi[:, lanes])
            acc += dot(slo[...], vhi[:, lanes])
            acc += dot(shi[...], vlo[:, lanes])
            part[q, :, :, :, :, lanes] = acc.reshape(2, 2, 4, ROWS, 256)
            return 0

        lax.fori_loop(0, 4, tile, 0)
        for dx in (1, 2, 3):
            there = lax.rem(x + dx, 4)
            remote(
                part.at[q, :, :, there], xr.at[q, dx - 1], x_ss.at[q], x_rs.at[q],
                (zlo * 4 + there, col),
            ).start()

    def rx(q):
        drain(xr.at[q], x_rs.at[q])
        for side in (1, 0):
            z = lax.rem(zlo + side, 2)
            for k in range(2):
                zb[q, side, k] = (
                    (part[q, k, z, x] + xr[q, 0, k, z]) + (xr[q, 1, k, z] + xr[q, 2, k, z])
                )
            if side:
                remote(zb.at[q, 1], zr.at[q], z_ss.at[q], z_rs.at[q], dev_zlo).start()

    def out_rows(k, z, q):
        return pl.ds(pl.multiple_of(k * 128 + 64 * z + q * ROWS, 8), ROWS)

    def rz(q):
        drain(zr.at[q], z_rs.at[q])
        tiles = []
        for k in range(2):
            rows = out_rows(k, zlo, q)
            for al in range(8):
                lanes = slice(al * 128, (al + 1) * 128)
                denom = (evir_s[0, col * 8 + al] + evir_v[...]) - occ[rows, :]
                value = (zb[q, 0, k, :, lanes] + zr[q, k, :, lanes]) / denom
                out[rows, lanes] = value
                tiles.append(value)
        for bit in range(3):
            tiles = swap_bits(tiles, bit, bit)
        for bit in range(3):
            tiles = swap_bits(tiles, bit, bit + 3)
        tiles = swap_bits(tiles, 3, 6)
        for c in range(16):
            post_s[q, c] = tiles[c]
        for c in range(16):
            remote(
                post_s.at[q, c], post_r.at[q, col], o_ss.at[q], o_rs.at[q], (row_z, c)
            ).start()

    def fin(q):
        drain(post_r.at[q], o_rs.at[q])
        tiles = [post_r[q, c] for c in range(16)]
        for bit in range(3):
            tiles = swap_bits(tiles, bit, bit + 3)
        tiles = swap_bits(tiles, 3, 6)
        for k in range(2):
            for bl in range(8):
                out[out_rows(k, 1 - zlo, q), bl * 128 : (bl + 1) * 128] = tiles[k * 8 + bl]

    def when(stage, q):
        if 0 <= q < ROUNDS:
            stage(q)

    for i in range(ROUNDS + 3):
        when(g1, i)
        if i + 2 < ROUNDS:
            pre_send(i + 2)
        when(rz, i - 3)
        if i == 0:
            lax.fori_loop(0, 16, convert, 0)
        when(g4, i - 1)
        when(g2, i)
        when(mm, i - 1)
        when(rx, i - 2)
        when(g3, i)
        when(fin, i - 3)

    for q in range(ROUNDS):
        drain(pre_s.at[q], pre_ss.at[q])
        drain(slab.at[q, 0, pl.ds(0, 7)], g_ss.at[q])
        drain(slab.at[q, 0], c_ss.at[q])
        drain(xr.at[q], x_ss.at[q])
        drain(zr.at[q], z_ss.at[q])
        drain(post_s.at[q], o_ss.at[q])


def on_device(amplitudes, integrals, amp_mask, int_mask, pairs, eps_occ, eps_vir):
    vmem = pl.BlockSpec(memory_space=pltpu.VMEM)
    smem = pl.BlockSpec(memory_space=pltpu.SMEM)
    hbm = pl.BlockSpec(memory_space=pl.ANY)
    dma = pltpu.SemaphoreType.DMA
    n = ROUNDS
    eps_vir = eps_vir.reshape(1, 128)
    return pl.pallas_call(
        kernel,
        out_shape=jax.ShapeDtypeStruct((256, 1024), F32),
        in_specs=[hbm, hbm, smem, smem, vmem, vmem, vmem, vmem, smem],
        out_specs=vmem,
        scratch_shapes=[
            pltpu.VMEM((128, 2048), F32),
            pltpu.VMEM((2048, 1024), F32),
            pltpu.VMEM((2048, 1024), BF16),
            pltpu.VMEM((2048, 1024), BF16),
            pltpu.VMEM((n, 8, 2, ROWS, 128), F32),
            pltpu.VMEM((n, 8, 2, ROWS, 128), F32),
            pltpu.VMEM((n, 2, 8, ROWS, 2048), F32),
            pltpu.VMEM((16 * ROWS, 2048), BF16),
            pltpu.VMEM((16 * ROWS, 2048), BF16),
            pltpu.VMEM((n, 2, 2, 4, ROWS, 1024), F32),
            pltpu.VMEM((n, 3, 2, 2, ROWS, 1024), F32),
            pltpu.VMEM((n, 2, 2, ROWS, 1024), F32),
            pltpu.VMEM((n, 2, ROWS, 1024), F32),
            pltpu.VMEM((n, 16, ROWS, 128), F32),
            pltpu.VMEM((n, 16, ROWS, 128), F32),
            pltpu.VMEM((256, 128), F32),
            pltpu.VMEM((128, 128), F32),
            dma((17,)),
            dma((n,)), dma((n,)),
            dma((n,)), dma((n, 9)),
            dma((n,)), dma((n,)),
            dma((n,)), dma((n,)),
            dma((n,)), dma((n,)),
            dma((n,)), dma((n,)),
        ],
        compiler_params=pltpu.CompilerParams(
            collective_id=0, has_side_effects=True, vmem_limit_bytes=60 * 2**20
        ),
        cost_estimate=pl.CostEstimate(
            flops=3 * 2 * 1024 * 2048 * 1024, bytes_accessed=10 * 2**20, transcendentals=0
        ),
        name="ladder",
    )(
        amplitudes, integrals, amp_mask, int_mask, int_mask, pairs,
        eps_occ.reshape(1, 200), eps_vir, eps_vir,
    )


def solution(mesh):
    return jax.shard_map(
        on_device,
        mesh=mesh,
        in_specs=(P("col", "row"), P("row", "col"), P(), P(), P("row", None), P(), P()),
        out_specs=P("row", "col"),
        check_vma=False,
    )
```

```python
import functools

import jax
import jax.numpy as jnp
from jax import lax
from jax.experimental import pallas as pl
from jax.experimental.pallas import tpu as pltpu
from jax.sharding import PartitionSpec as P

MESH = pl.DeviceIdType.MESH
ROUNDS = 8
ROWS = 64 // ROUNDS
F32 = jnp.float32
BF16 = jnp.bfloat16
Y_FIRST = frozenset((1, 3, 5,))
ORDER = (
    ("P", 0), ("P", 1), ("P", 2), ("P", 3), ("C", 0), ("P", 4), ("C", 1), ("G1", 0), ("G1", 1),
    ("G1", 2), ("G2a", 0), ("G2b", 0), ("G2a", 1), ("G2b", 1), ("G1", 3), ("G2a", 2), ("G3a", 0),
    ("G3b", 0), ("P", 5), ("C", 2), ("G2b", 2), ("G3a", 1), ("G1", 4), ("C", 3), ("G3a", 2),
    ("P", 6), ("G4", 0), ("G2a", 3), ("G3b", 1), ("MA", 0), ("G4", 1), ("G2b", 3), ("G3b", 2),
    ("MB", 0), ("G1", 5), ("P", 7), ("MA", 1), ("G2a", 4), ("G4", 2), ("G3a", 3), ("MB", 1),
    ("G2b", 4), ("G3b", 3), ("X1", 0), ("G2a", 5), ("G1", 6), ("MA", 2), ("MB", 2), ("G4", 3),
    ("G3a", 4), ("G3b", 4), ("X1", 1), ("G2b", 5), ("G1", 7), ("G3a", 5), ("MA", 3), ("G2a", 6),
    ("G4", 4), ("MB", 3), ("G2b", 6), ("G3b", 5), ("X1", 2), ("G2a", 7), ("G2b", 7), ("X", 0),
    ("MA", 4), ("G4", 5), ("MB", 4), ("X", 1), ("X1", 3), ("G3a", 6), ("G3a", 7), ("G3b", 6),
    ("MA", 5), ("G3b", 7), ("MB", 5), ("G4", 6), ("X", 2), ("X1", 4), ("Z", 0), ("G4", 7),
    ("MA", 6), ("MB", 6), ("MA", 7), ("MB", 7), ("X", 3), ("X", 4), ("F", 0), ("X1", 5),
    ("X1", 6), ("Z", 1), ("Z", 2), ("X1", 7), ("Z", 3), ("X", 5), ("X", 6), ("X", 7), ("Z", 4),
    ("Z", 5), ("Z", 6), ("Z", 7), ("F", 1), ("F", 2), ("F", 3), ("F", 4), ("F", 5), ("F", 6),
    ("F", 7),
)


def swap_bits(tiles, tile_bit, lane_bit):
    step = 1 << lane_bit
    lane = lax.broadcasted_iota(jnp.int32, tiles[0].shape, len(tiles[0].shape) - 1)
    upper = (lane & step) != 0
    result = list(tiles)
    for low in range(len(tiles)):
        if low >> tile_bit & 1:
            continue
        high = low | 1 << tile_bit
        a, b = tiles[low], tiles[high]
        result[low] = jnp.where(upper, pltpu.roll(b, step, 1), a)
        result[high] = jnp.where(upper, b, pltpu.roll(a, 128 - step, 1))
    return result


def split(value):
    hi = value.astype(BF16)
    return hi, (value - hi.astype(F32)).astype(BF16)


def kernel(
    t_hbm, v_hbm, am_s, im_s, im_v, pairs_v, eocc_v, evir_v, evir_s,
    out,
    tbuf, vbuf, vhi, vlo, pre_s, pre_r, slab, terms, part, xa, xf, zb, zr, post_s, post_r, occ, imf,
    load_sem, pre_ss, pre_rs, g_ss, g_rs, c_ss, c_rs, x_ss, xa_rs, xf_rs, z_ss, z_rs, o_ss, o_rs,
):
    row = lax.axis_index("row")
    col = lax.axis_index("col")
    zlo, x = row // 4, lax.rem(row, 4)
    y, zhi, core = col // 4, lax.rem(col // 2, 2), lax.rem(col, 2)
    chip = col // 2
    row_z = lax.rem(row + 4, 8)
    col_far = lax.rem(col + 8, 16)
    up = lax.rem(y + 1, 4)
    down = lax.rem(y + 3, 4)
    opposite = lax.rem(y + 2, 4)
    flip = 1 - zhi

    def col_of(yy, zz):
        return yy * 4 + zz * 2 + core

    dev_up = (row, col_of(up, zhi))
    dev_down = (row, col_of(down, zhi))
    dev_z = (row, col_of(y, flip))
    dev_core = (row, chip * 2 + 1 - core)
    dev_zlo = (row_z, col)
    right, left, across = lax.rem(x + 1, 4), lax.rem(x + 3, 4), lax.rem(x + 2, 4)
    dev_right = (zlo * 4 + right, col)
    dev_left = (zlo * 4 + left, col)
    own_off = 64 * (y // 2)
    send_off = 64 - own_off

    barrier = pltpu.get_barrier_semaphore()
    peers = [(r, col_far) for r in range(8)]
    peers += [dev_up, dev_down, dev_z, dev_core]
    peers += [dev_right, dev_left]
    peers += [(row_z, lax.rem(col + j, 16)) for j in range(16) if j != 8]
    for peer in peers:
        pl.semaphore_signal(barrier, inc=1, device_id=peer, device_id_type=MESH)

    def t_load(offset, which):
        rows = pl.ds(pl.multiple_of(offset, 8), 64)
        return pltpu.make_async_copy(t_hbm.at[rows], tbuf.at[rows], load_sem.at[which])

    t_load(send_off, 16).start()
    t_load(own_off, 17).start()

    def v_load(block):
        rows = pl.ds(block * 128, 128)
        return pltpu.make_async_copy(v_hbm.at[rows], vbuf.at[rows], load_sem.at[block])

    for block in range(16):
        v_load(block).start()

    def remote(src, dst, send_sem, recv_sem, device):
        return pltpu.make_async_remote_copy(
            src_ref=src, dst_ref=dst, send_sem=send_sem, recv_sem=recv_sem,
            device_id=device, device_id_type=MESH,
        )

    def drain(ref, sem):
        pltpu.make_async_copy(ref, ref, sem).wait()

    imf[...] = im_v[...].astype(F32)

    ids = lax.broadcasted_iota(jnp.int32, (128, 128), 1)
    for block in range(2):
        rows = slice(block * 128, (block + 1) * 128)
        total = []
        for j in range(2):
            picked = jnp.transpose(jnp.broadcast_to(pairs_v[j : j + 1, rows], (128, 128)))
            total.append(
                jnp.sum(jnp.where(picked == ids, eocc_v[:, 0:128], 0.0), axis=1, keepdims=True)
                + jnp.sum(
                    jnp.where(picked[:, 0:72] == ids[:, 0:72] + 128, eocc_v[:, 128:200], 0.0),
                    axis=1, keepdims=True,
                )
            )
        occ[rows, :] = jnp.broadcast_to(total[0] + total[1], (128, 128))

    t_load(send_off, 16).wait()

    def masked_tile(offset, q, j):
        rows = pl.ds(pl.multiple_of(offset + q * ROWS, 8), ROWS)
        return tbuf[rows, j * 128 : (j + 1) * 128] * am_s[col, row * 16 + j].astype(F32)

    def pre_shuffle(q):
        tiles = [masked_tile(send_off, q, j) for j in range(16)]
        for bit in range(4):
            tiles = swap_bits(tiles, bit, bit)
        for bit in range(3):
            tiles = swap_bits(tiles, bit, bit + 4)
        for j in range(16):
            pre_s[q, j % 8, j // 8] = tiles[j]

    def pre_send(q):
        for r in range(8):
            remote(
                pre_s.at[q, r], pre_r.at[q, row], pre_ss.at[q], pre_rs.at[q], (r, col_far)
            ).start()

    for q in range(ROUNDS):
        pre_shuffle(q)
    pl.semaphore_wait(barrier, len(peers))
    t_load(own_off, 17).wait()

    def convert(block, _):
        v_load(block).wait()
        rows = pl.ds(pl.multiple_of(block * 128, 128), 128)
        for al in range(8):
            lanes = slice(al * 128, (al + 1) * 128)
            weight = im_s[row * 16 + block, col * 8 + al].astype(F32)
            hi, lo = split(vbuf[rows, lanes] * imf[...] * weight)
            vhi[rows, lanes] = hi
            vlo[rows, lanes] = lo
        return 0

    def slot(q, yy, zz, lanes=None):
        ref = slab.at[q, core, yy * 2 + zz]
        return ref if lanes is None else ref.at[:, lanes]

    LOWER, UPPER = pl.ds(0, 1024), pl.ds(1024, 1024)

    def push(q, kind, yy, zz, device, lanes=None):
        ref = slot(q, yy, zz, lanes)
        remote(ref, ref, g_ss.at[q], g_rs.at[q, kind], device).start()

    def arrived(q, kind, yy, zz, lanes=None):
        drain(slot(q, yy, zz, lanes), g_rs.at[q, kind])

    def to_core(q, yy, zz):
        ref = slot(q, yy, zz)
        remote(ref, ref, c_ss.at[q], c_rs.at[q], dev_core).start()

    def g1(q):
        drain(pre_r.at[q], pre_rs.at[q])
        tiles = [pre_r[q, j % 8, j // 8] for j in range(16)]
        for bit in range(3):
            tiles = swap_bits(tiles, bit, bit + 4)
        for j in range(16):
            slab[q, core, chip, :, j * 128 : (j + 1) * 128] = masked_tile(own_off, q, j) + tiles[j]
        push(q, 1, y, zhi, dev_up)
        push(q, 2, y, zhi, dev_down)
        push(q, 0, y, zhi, dev_z)
        to_core(q, y, zhi)

    def g2a(q):
        arrived(q, 1, down, zhi)
        push(q, 3, down, zhi, dev_up, LOWER)
        arrived(q, 2, up, zhi)
        push(q, 4, up, zhi, dev_down, UPPER)
        if q in Y_FIRST:
            push(q, 5, down, zhi, dev_z)
            push(q, 6, up, zhi, dev_z)
        to_core(q, down, zhi)
        to_core(q, up, zhi)

    def g2b(q):
        arrived(q, 0, y, flip)
        if q not in Y_FIRST:
            push(q, 5, y, flip, dev_up)
            push(q, 6, y, flip, dev_down)
        to_core(q, y, flip)

    def g3a(q):
        arrived(q, 3, opposite, zhi, LOWER)
        arrived(q, 4, opposite, zhi, UPPER)
        if q in Y_FIRST:
            push(q, 7, opposite, zhi, dev_z)
        to_core(q, opposite, zhi)

    def g3b(q):
        arrived(q, 5, down, flip)
        if q not in Y_FIRST:
            push(q, 7, down, flip, dev_up, LOWER)
        arrived(q, 6, up, flip)
        if q not in Y_FIRST:
            push(q, 8, up, flip, dev_down, UPPER)
        to_core(q, down, flip)
        to_core(q, up, flip)

    def g4(q):
        if q in Y_FIRST:
            arrived(q, 7, opposite, flip)
        else:
            arrived(q, 7, opposite, flip, LOWER)
            arrived(q, 8, opposite, flip, UPPER)
        to_core(q, opposite, flip)

    def tile(q, n):
        lanes = slice(n * 512, (n + 1) * 512)
        dot = functools.partial(jnp.dot, preferred_element_type=F32)
        both = dot(terms[q % 2], vhi[:, lanes])
        acc = (both[:128] + both[128:]) + dot(terms[q % 2, :128], vlo[:, lanes])
        part[q, :, :, :, :, lanes] = acc.reshape(2, 2, 4, ROWS, 512)
        onward, back = (dev_right, dev_left) if n == 0 else (dev_left, dev_right)
        near = left if n == 0 else right
        remote(
            part.at[q, :, :, across, :, lanes], xa.at[q, n], x_ss.at[q], xa_rs.at[q, n], onward
        ).start()
        remote(
            part.at[q, :, :, near, :, lanes], xf.at[q, n], x_ss.at[q], xf_rs.at[q], back
        ).start()

    def ma(q):
        drain(slab.at[q, 0], c_rs.at[q])
        for k in range(2):
            for c in range(0, 8, 2):
                hi, lo = split(slab[q, k, c : c + 2].reshape(16, 2048))
                at = (k * 8 + c) * ROWS
                terms[q % 2, at : at + 16, :] = hi
                terms[q % 2, 128 + at : 144 + at, :] = lo
        tile(q, 0)

    def mb(q):
        tile(q, 1)

    def x1(q):
        for n in range(2):
            lanes = slice(n * 512, (n + 1) * 512)
            onward, near = (dev_right, right) if n == 0 else (dev_left, left)
            drain(xa.at[q, n], xa_rs.at[q, n])
            for k in range(2):
                for z in range(2):
                    xa[q, n, k, z] = xa[q, n, k, z] + part[q, k, z, near, :, lanes]
            remote(xa.at[q, n], xf.at[q, 2 + n], x_ss.at[q], xf_rs.at[q], onward).start()

    def rx(q):
        drain(xf.at[q], xf_rs.at[q])
        for side in (1, 0):
            z = lax.rem(zlo + side, 2)
            for k in range(2):
                for n in range(2):
                    lanes = slice(n * 512, (n + 1) * 512)
                    zb[q, side, k, :, lanes] = (part[q, k, z, x, :, lanes] + xf[q, n, k, z]) + xf[
                        q, 2 + n, k, z
                    ]
            if side:
                remote(zb.at[q, 1], zr.at[q], z_ss.at[q], z_rs.at[q], dev_zlo).start()

    def out_rows(k, z, q):
        return pl.ds(pl.multiple_of(k * 128 + 64 * z + q * ROWS, 8), ROWS)

    def rz(q):
        drain(zr.at[q], z_rs.at[q])
        tiles = []
        for k in range(2):
            rows = out_rows(k, zlo, q)
            for al in range(8):
                lanes = slice(al * 128, (al + 1) * 128)
                denom = (evir_s[0, col * 8 + al] + evir_v[...]) - occ[rows, :]
                value = (zb[q, 0, k, :, lanes] + zr[q, k, :, lanes]) / denom
                out[rows, lanes] = value
                tiles.append(value)
        for bit in range(3):
            tiles = swap_bits(tiles, bit, bit)
        for bit in range(3):
            tiles = swap_bits(tiles, bit, bit + 3)
        tiles = swap_bits(tiles, 3, 6)
        for c in range(16):
            post_s[q, c] = tiles[c]
        for c in range(16):
            remote(
                post_s.at[q, c], post_r.at[q, col], o_ss.at[q], o_rs.at[q], (row_z, c)
            ).start()

    def fin(q):
        drain(post_r.at[q], o_rs.at[q])
        tiles = [post_r[q, c] for c in range(16)]
        for bit in range(3):
            tiles = swap_bits(tiles, bit, bit + 3)
        tiles = swap_bits(tiles, 3, 6)
        for k in range(2):
            for bl in range(8):
                out[out_rows(k, 1 - zlo, q), bl * 128 : (bl + 1) * 128] = tiles[k * 8 + bl]

    def convert_four(i):
        lax.fori_loop(4 * i, 4 * i + 4, convert, 0)

    stages = {
        "P": pre_send, "C": convert_four, "G1": g1, "G2a": g2a, "G2b": g2b, "G3a": g3a,
        "G3b": g3b, "G4": g4, "MA": ma, "MB": mb, "X1": x1, "X": rx, "Z": rz, "F": fin,
    }
    for stage, q in ORDER:
        stages[stage](q)

    for q in range(ROUNDS):
        drain(pre_s.at[q], pre_ss.at[q])
        drain(slab.at[q, 0, pl.ds(0, 7)], g_ss.at[q])
        drain(slab.at[q, 0], c_ss.at[q])
        drain(xf.at[q], x_ss.at[q])
        drain(xa.at[q], x_ss.at[q])
        drain(zr.at[q], z_ss.at[q])
        drain(post_s.at[q], o_ss.at[q])


def on_device(amplitudes, integrals, amp_mask, int_mask, pairs, eps_occ, eps_vir):
    vmem = pl.BlockSpec(memory_space=pltpu.VMEM)
    smem = pl.BlockSpec(memory_space=pltpu.SMEM)
    hbm = pl.BlockSpec(memory_space=pl.ANY)
    dma = pltpu.SemaphoreType.DMA
    n = ROUNDS
    eps_vir = eps_vir.reshape(1, 128)
    return pl.pallas_call(
        kernel,
        out_shape=pltpu.VMEM((256, 1024), F32),
        in_specs=[hbm, hbm, smem, smem, vmem, vmem, vmem, vmem, smem],
        out_specs=vmem,
        scratch_shapes=[
            pltpu.VMEM((128, 2048), F32),
            pltpu.VMEM((2048, 1024), F32),
            pltpu.VMEM((2048, 1024), BF16),
            pltpu.VMEM((2048, 1024), BF16),
            pltpu.VMEM((n, 8, 2, ROWS, 128), F32),
            pltpu.VMEM((n, 8, 2, ROWS, 128), F32),
            pltpu.VMEM((n, 2, 8, ROWS, 2048), F32),
            pltpu.VMEM((2, 32 * ROWS, 2048), BF16),
            pltpu.VMEM((n, 2, 2, 4, ROWS, 1024), F32),
            pltpu.VMEM((n, 2, 2, 2, ROWS, 512), F32),
            pltpu.VMEM((n, 4, 2, 2, ROWS, 512), F32),
            pltpu.VMEM((n, 2, 2, ROWS, 1024), F32),
            pltpu.VMEM((n, 2, ROWS, 1024), F32),
            pltpu.VMEM((n, 16, ROWS, 128), F32),
            pltpu.VMEM((n, 16, ROWS, 128), F32),
            pltpu.VMEM((256, 128), F32),
            pltpu.VMEM((128, 128), F32),
            dma((18,)),
            dma((n,)), dma((n,)),
            dma((n,)), dma((n, 9)),
            dma((n,)), dma((n,)),
            dma((n,)), dma((n, 2)), dma((n,)),
            dma((n,)), dma((n,)),
            dma((n,)), dma((n,)),
        ],
        compiler_params=pltpu.CompilerParams(
            collective_id=0, has_side_effects=True, vmem_limit_bytes=60 * 2**20
        ),
        cost_estimate=pl.CostEstimate(
            flops=3 * 2 * 1024 * 2048 * 1024, bytes_accessed=10 * 2**20, transcendentals=0
        ),
        name="ladder",
    )(
        amplitudes, integrals, amp_mask, int_mask, int_mask, pairs.T,
        eps_occ.reshape(1, 200), eps_vir, eps_vir,
    )


def solution(mesh):
    return jax.shard_map(
        on_device,
        mesh=mesh,
        in_specs=(P("col", "row"), P("row", "col"), P(), P(), P("row", None), P(), P()),
        out_specs=P("row", "col"),
        check_vma=False,
    )
```

```python
import functools

import jax
import jax.numpy as jnp
from jax import lax
from jax.experimental import pallas as pl
from jax.experimental.pallas import tpu as pltpu
from jax.sharding import PartitionSpec as P

MESH = pl.DeviceIdType.MESH
ROUNDS = 8
ROWS = 64 // ROUNDS
F32 = jnp.float32
BF16 = jnp.bfloat16
Y_FIRST = frozenset((0, 3, 5,))
EARLY = (6, 7,)
ORDER = (
    ("P", 0), ("P", 1), ("P", 2), ("P", 3), ("C", 0), ("C", 1), ("P", 4), ("G1", 0), ("G1", 1),
    ("G1", 2), ("C", 2), ("C", 3), ("G2a", 0), ("G1", 3), ("G2a", 1), ("G2a", 2), ("G2b", 0),
    ("G2b", 1), ("G3a", 0), ("G2b", 2), ("P", 5), ("G3a", 1), ("G2a", 3), ("MA", 0), ("G3b", 0),
    ("G3a", 2), ("G3b", 1), ("P", 6), ("MA", 1), ("G4", 0), ("G1", 4), ("G3b", 2), ("P", 7),
    ("MA", 2), ("G4", 1), ("MB", 0), ("G3a", 3), ("G2b", 3), ("X1A", 0), ("G1", 5), ("G2b", 4),
    ("MB", 1), ("G1", 6), ("G4", 2), ("G2a", 4), ("MA", 3), ("X1A", 1), ("X1B", 0), ("G3b", 3),
    ("G4", 3), ("G1", 7), ("G2a", 5), ("X1A", 2), ("XA", 0), ("MB", 2), ("G2a", 6), ("X1A", 3),
    ("G2b", 5), ("G3a", 4), ("G3b", 4), ("G2b", 6), ("MB", 3), ("XA", 1), ("XB", 0), ("X1B", 1),
    ("G3a", 5), ("MA", 4), ("X1B", 2), ("G4", 4), ("XA", 2), ("G3a", 6), ("G2b", 7), ("MA", 5),
    ("G3b", 5), ("G3b", 6), ("X1B", 3), ("G2a", 7), ("MB", 4), ("X1A", 4), ("XA", 3), ("ZA", 0),
    ("ZA", 1), ("XB", 1), ("G4", 5), ("MA", 6), ("G4", 6), ("G3b", 7), ("XB", 2), ("G3a", 7),
    ("X1A", 5), ("ZA", 2), ("MB", 5), ("X1B", 4), ("MB", 6), ("XB", 3), ("ZB", 0), ("G4", 7),
    ("XA", 4), ("MA", 7), ("X1B", 5), ("XA", 5), ("ZB", 1), ("ZA", 3), ("X1A", 6), ("MB", 7),
    ("XB", 4), ("ZA", 4), ("ZB", 2), ("ZB", 3), ("X1A", 7), ("ZA", 5), ("X1B", 6), ("XB", 5),
    ("XA", 6), ("X1B", 7), ("ZB", 4), ("XA", 7), ("F", 0), ("XB", 6), ("F", 1), ("F", 2),
    ("F", 3), ("ZA", 6), ("ZB", 5), ("XB", 7), ("F", 4), ("ZA", 7), ("F", 5), ("ZB", 6), ("F", 6),
    ("ZB", 7), ("F", 7),
)


def swap_bits(tiles, tile_bit, lane_bit):
    step = 1 << lane_bit
    lane = lax.broadcasted_iota(jnp.int32, tiles[0].shape, len(tiles[0].shape) - 1)
    upper = (lane & step) != 0
    result = list(tiles)
    for low in range(len(tiles)):
        if low >> tile_bit & 1:
            continue
        high = low | 1 << tile_bit
        a, b = tiles[low], tiles[high]
        result[low] = jnp.where(upper, pltpu.roll(b, step, 1), a)
        result[high] = jnp.where(upper, b, pltpu.roll(a, 128 - step, 1))
    return result


def split(value):
    hi = value.astype(BF16)
    return hi, (value - hi.astype(F32)).astype(BF16)


def kernel(
    t_hbm, v_hbm, am_s, im_s, im_v, pairs_v, eocc_v, evir_v, evir_s,
    out,
    tbuf, vbuf, vhi, vlo, pre_s, pre_r, slab, terms, part, xa, xf, zb, zr, post_s, post_r, twin_s, twin_r, occ, imf,
    load_sem, pre_ss, pre_rs, g_ss, g_rs, c_ss, c_rs, x_ss, xa_rs, xf_rs, z_ss, z_rs, o_ss, o_rs,
):
    row = lax.axis_index("row")
    col = lax.axis_index("col")
    zlo, x = row // 4, lax.rem(row, 4)
    y, zhi, core = col // 4, lax.rem(col // 2, 2), lax.rem(col, 2)
    chip = col // 2
    row_z = lax.rem(row + 4, 8)
    col_far = lax.rem(col + 8, 16)
    up = lax.rem(y + 1, 4)
    down = lax.rem(y + 3, 4)
    opposite = lax.rem(y + 2, 4)
    flip = 1 - zhi

    def col_of(yy, zz):
        return yy * 4 + zz * 2 + core

    dev_up = (row, col_of(up, zhi))
    dev_down = (row, col_of(down, zhi))
    dev_z = (row, col_of(y, flip))
    dev_core = (row, chip * 2 + 1 - core)
    dev_zlo = (row_z, col)
    right, left, across = lax.rem(x + 1, 4), lax.rem(x + 3, 4), lax.rem(x + 2, 4)
    dev_right = (zlo * 4 + right, col)
    dev_left = (zlo * 4 + left, col)
    own_off = 64 * (y // 2)
    send_off = 64 - own_off

    barrier = pltpu.get_barrier_semaphore()
    peers = [(r, col_far) for r in range(8)]
    peers += [(row, lax.rem(col + j, 16)) for j in range(1, 16)]
    peers += [dev_right, dev_left]
    peers += [(row_z, lax.rem(col + j, 16)) for j in range(16) if j != 8]
    for peer in peers:
        pl.semaphore_signal(barrier, inc=1, device_id=peer, device_id_type=MESH)

    def t_load(offset, count, which):
        rows = pl.ds(pl.multiple_of(offset, 8), count)
        return pltpu.make_async_copy(t_hbm.at[rows], tbuf.at[rows], load_sem.at[which])

    t_first = t_load(send_off, 2 * ROWS, 16)
    t_rest = t_load(send_off + 2 * ROWS, 64 - 2 * ROWS, 17)
    t_own = t_load(own_off, 64, 18)
    for load in (t_first, t_rest, t_own):
        load.start()

    def v_load(block):
        rows = pl.ds(block * 128, 128)
        return pltpu.make_async_copy(v_hbm.at[rows], vbuf.at[rows], load_sem.at[block])

    for block in range(16):
        v_load(block).start()

    def remote(src, dst, send_sem, recv_sem, device):
        return pltpu.make_async_remote_copy(
            src_ref=src, dst_ref=dst, send_sem=send_sem, recv_sem=recv_sem,
            device_id=device, device_id_type=MESH,
        )

    def drain(ref, sem):
        pltpu.make_async_copy(ref, ref, sem).wait()


    def masked_tile(offset, q, j):
        rows = pl.ds(pl.multiple_of(offset + q * ROWS, 8), ROWS)
        return tbuf[rows, j * 128 : (j + 1) * 128] * am_s[col, row * 16 + j].astype(F32)

    def pre_shuffle(q):
        tiles = [masked_tile(send_off, q, j) for j in range(16)]
        for bit in range(4):
            tiles = swap_bits(tiles, bit, bit)
        for bit in range(3):
            tiles = swap_bits(tiles, bit, bit + 4)
        for j in range(16):
            pre_s[q, j % 8, j // 8] = tiles[j]

    def pre_send(q):
        if q == 2:
            t_rest.wait()
        if q >= 2:
            pre_shuffle(q)
        for r in range(8):
            remote(
                pre_s.at[q, r], pre_r.at[q, row], pre_ss.at[q], pre_rs.at[q], (r, col_far)
            ).start()

    t_first.wait()
    pre_shuffle(0)
    pre_shuffle(1)
    pl.semaphore_wait(barrier, len(peers))

    def constants():
        imf[...] = im_v[...].astype(F32)

        ids = lax.broadcasted_iota(jnp.int32, (128, 128), 1)
        for block in range(2):
            rows = slice(block * 128, (block + 1) * 128)
            total = []
            for j in range(2):
                picked = jnp.transpose(jnp.broadcast_to(pairs_v[j : j + 1, rows], (128, 128)))
                total.append(
                    jnp.sum(jnp.where(picked == ids, eocc_v[:, 0:128], 0.0), axis=1, keepdims=True)
                    + jnp.sum(
                        jnp.where(picked[:, 0:72] == ids[:, 0:72] + 128, eocc_v[:, 128:200], 0.0),
                        axis=1, keepdims=True,
                    )
                )
            occ[rows, :] = jnp.broadcast_to(total[0] + total[1], (128, 128))

    def convert(block, _):
        v_load(block).wait()
        rows = pl.ds(pl.multiple_of(block * 128, 128), 128)
        for al in range(8):
            lanes = slice(al * 128, (al + 1) * 128)
            weight = im_s[row * 16 + block, col * 8 + al].astype(F32)
            hi, lo = split(vbuf[rows, lanes] * imf[...] * weight)
            vhi[rows, lanes] = hi
            vlo[rows, lanes] = lo
        return 0

    def slot(q, yy, zz, lanes=None):
        ref = slab.at[q, core, yy, zz]
        return ref if lanes is None else ref.at[:, lanes]

    LOWER, UPPER = pl.ds(0, 1024), pl.ds(1024, 1024)

    def push(q, kind, yy, zz, device, lanes=None):
        ref = slot(q, yy, zz, lanes)
        remote(ref, ref, g_ss.at[q], g_rs.at[q, kind], device).start()

    def arrived(q, kind, yy, zz, lanes=None):
        drain(slot(q, yy, zz, lanes), g_rs.at[q, kind])

    def to_core(q, yy, zz):
        ref = slot(q, yy, zz)
        half = 0 if zz is zhi else 1
        remote(ref, ref, c_ss.at[q], c_rs.at[q, half], dev_core).start()

    def g1(q):
        if q == 0:
            t_own.wait()
        drain(pre_r.at[q], pre_rs.at[q])
        tiles = [pre_r[q, j % 8, j // 8] for j in range(16)]
        for bit in range(3):
            tiles = swap_bits(tiles, bit, bit + 4)
        for j in range(16):
            slab[q, core, y, zhi, :, j * 128 : (j + 1) * 128] = masked_tile(own_off, q, j) + tiles[j]
        push(q, 1, y, zhi, dev_up)
        push(q, 2, y, zhi, dev_down)
        push(q, 0, y, zhi, dev_z)
        to_core(q, y, zhi)

    def g2a(q):
        arrived(q, 1, down, zhi)
        push(q, 3, down, zhi, dev_up, LOWER)
        arrived(q, 2, up, zhi)
        push(q, 4, up, zhi, dev_down, UPPER)
        if q in Y_FIRST:
            push(q, 5, down, zhi, dev_z)
            push(q, 6, up, zhi, dev_z)
        to_core(q, down, zhi)
        to_core(q, up, zhi)

    def g2b(q):
        arrived(q, 0, y, flip)
        if q not in Y_FIRST:
            push(q, 5, y, flip, dev_up)
            push(q, 6, y, flip, dev_down)
        to_core(q, y, flip)

    def g3a(q):
        arrived(q, 3, opposite, zhi, LOWER)
        arrived(q, 4, opposite, zhi, UPPER)
        if q in Y_FIRST:
            push(q, 7, opposite, zhi, dev_z)
        to_core(q, opposite, zhi)

    def g3b(q):
        arrived(q, 5, down, flip)
        if q not in Y_FIRST:
            push(q, 7, down, flip, dev_up, LOWER)
        arrived(q, 6, up, flip)
        if q not in Y_FIRST:
            push(q, 8, up, flip, dev_down, UPPER)
        to_core(q, down, flip)
        to_core(q, up, flip)

    def g4(q):
        if q in Y_FIRST:
            arrived(q, 7, opposite, flip)
        else:
            arrived(q, 7, opposite, flip, LOWER)
            arrived(q, 8, opposite, flip, UPPER)
        to_core(q, opposite, flip)

    parity = lax.rem(x, 2)

    def mm(q, plane, half):
        drain(slab.at[q, 0, pl.ds(0, 2)], c_rs.at[q, half])
        for k in range(2):
            for yy in range(0, 4, 2):
                value = jnp.concatenate([slab[q, k, yy, plane], slab[q, k, yy + 1, plane]], axis=0)
                hi, lo = split(value)
                at = (k * 4 + yy) * ROWS
                terms[half, at : at + 16, :] = hi
                terms[half, 64 + at : 80 + at, :] = lo
        for n in range(2):
            lanes = slice(n * 512, (n + 1) * 512)
            dot = functools.partial(jnp.dot, preferred_element_type=F32)
            both = dot(terms[half], vhi[:, lanes])
            acc = (both[:64] + both[64:]) + dot(terms[half, :64], vlo[:, lanes])
            part[q, plane, :, :, :, :, lanes] = acc.reshape(2, 2, 2, ROWS, 512)
            onward, back = (dev_right, dev_left) if n == 0 else (dev_left, dev_right)
            near = left if n == 0 else right

            @pl.when(parity == plane)
            def _():
                remote(
                    part.at[q, plane, :, :, across // 2, :, lanes], xa.at[q, n], x_ss.at[q],
                    xa_rs.at[q, n], onward,
                ).start()

            @pl.when(parity != plane)
            def _():
                remote(
                    part.at[q, plane, :, :, near // 2, :, lanes], xf.at[q, n], x_ss.at[q],
                    xf_rs.at[q], back,
                ).start()

    def join(q, plane):
        @pl.when(parity != plane)
        def _():
            for n in range(2):
                lanes = slice(n * 512, (n + 1) * 512)
                onward, near = (dev_right, right) if n == 0 else (dev_left, left)
                drain(xa.at[q, n], xa_rs.at[q, n])
                for k in range(2):
                    for z in range(2):
                        xa[q, n, k, z] = xa[q, n, k, z] + part[q, plane, k, z, near // 2, :, lanes]
                remote(xa.at[q, n], xf.at[q, 2 + n], x_ss.at[q], xf_rs.at[q], onward).start()

    def spread(tiles):
        for bit in range(3):
            tiles = swap_bits(tiles, bit, bit)
        for bit in range(3):
            tiles = swap_bits(tiles, bit, bit + 3)
        return swap_bits(tiles, 3, 6)

    def total(q, plane):
        @pl.when(parity == plane)
        def _():
            drain(xf.at[q], xf_rs.at[q])
            for side in (1, 0):
                z = lax.rem(zlo + side, 2)
                for k in range(2):
                    for n in range(2):
                        lanes = slice(n * 512, (n + 1) * 512)
                        zb[q, side, k, :, lanes] = (
                            part[q, plane, k, z, x // 2, :, lanes] + xf[q, n, k, z]
                        ) + xf[q, 2 + n, k, z]
                if side:
                    remote(zb.at[q, 1], zr.at[q], z_ss.at[q], z_rs.at[q], dev_zlo).start()
            if q in EARLY:
                e = EARLY.index(q)
                for side, there in ((0, row_z), (1, row)):
                    tiles = spread([
                        zb[q, side, k, :, al * 128 : (al + 1) * 128]
                        for k in range(2) for al in range(8)
                    ])
                    for c in range(16):
                        twin_s[e, side * 16 + c] = tiles[c]
                    for c in range(16):
                        copy = remote(
                            twin_s.at[e, side * 16 + c], twin_r.at[e, side * 16 + col],
                            o_ss.at[q], o_rs.at[q], (there, c),
                        )
                        if side:
                            pl.when(c != col)(copy.start)
                        else:
                            copy.start()
                twin_r[e, 16 + col] = twin_s[e, 16 + col]

    def out_rows(k, z, q):
        return pl.ds(pl.multiple_of(k * 128 + 64 * z + q * ROWS, 8), ROWS)

    def denominator(k, z, q, al):
        return (evir_s[0, col * 8 + al] + evir_v[...]) - occ[out_rows(k, z, q), :]

    def finish(q, plane):
        @pl.when(parity == plane)
        def _():
            drain(zr.at[q], z_rs.at[q])
            tiles = []
            for k in range(2):
                for al in range(8):
                    lanes = slice(al * 128, (al + 1) * 128)
                    value = zb[q, 0, k, :, lanes] + zr[q, k, :, lanes]
                    value = value / denominator(k, zlo, q, al)
                    out[out_rows(k, zlo, q), lanes] = value
                    tiles.append(value)
            if q not in EARLY:
                tiles = spread(tiles)
                for c in range(16):
                    post_s[q, c] = tiles[c]
                for c in range(16):
                    remote(
                        post_s.at[q, c], post_r.at[q, col], o_ss.at[q], o_rs.at[q], (row_z, c)
                    ).start()

    def fin(q):
        if q in EARLY:
            e = EARLY.index(q)
            drain(twin_r.at[e, pl.ds(0, 31)], o_rs.at[q])
            tiles = [twin_r[e, c] + twin_r[e, 16 + c] for c in range(16)]
        else:
            drain(post_r.at[q], o_rs.at[q])
            tiles = [post_r[q, c] for c in range(16)]
        for bit in range(3):
            tiles = swap_bits(tiles, bit, bit + 3)
        tiles = swap_bits(tiles, 3, 6)
        for k in range(2):
            for bl in range(8):
                value = tiles[k * 8 + bl]
                if q in EARLY:
                    value = value / denominator(k, 1 - zlo, q, bl)
                out[out_rows(k, 1 - zlo, q), bl * 128 : (bl + 1) * 128] = value

    def convert_four(i):
        if i == 0:
            constants()
        lax.fori_loop(4 * i, 4 * i + 4, convert, 0)

    stages = {
        "P": pre_send, "C": convert_four, "G1": g1, "G2a": g2a, "G2b": g2b, "G3a": g3a,
        "G3b": g3b, "G4": g4, "F": fin,
        "MA": lambda q: mm(q, zhi, 0), "MB": lambda q: mm(q, flip, 1),
        "X1A": lambda q: join(q, zhi), "X1B": lambda q: join(q, flip),
        "XA": lambda q: total(q, zhi), "XB": lambda q: total(q, flip),
        "ZA": lambda q: finish(q, zhi), "ZB": lambda q: finish(q, flip),
    }
    for stage, q in ORDER:
        stages[stage](q)

    for q in range(ROUNDS):
        drain(pre_s.at[q], pre_ss.at[q])
        drain(vbuf.at[pl.ds(0, 112)], g_ss.at[q])
        drain(slab.at[q, 0], c_ss.at[q])
        drain(vbuf.at[pl.ds(0, 96)], x_ss.at[q])
        drain(zr.at[q], z_ss.at[q])
        if q in EARLY:
            e = EARLY.index(q)
            drain(twin_s.at[e, pl.ds(0, 31)], o_ss.at[q])
        else:
            drain(post_s.at[q], o_ss.at[q])


def on_device(amplitudes, integrals, amp_mask, int_mask, pairs, eps_occ, eps_vir):
    vmem = pl.BlockSpec(memory_space=pltpu.VMEM)
    smem = pl.BlockSpec(memory_space=pltpu.SMEM)
    hbm = pl.BlockSpec(memory_space=pl.ANY)
    dma = pltpu.SemaphoreType.DMA
    n = ROUNDS
    eps_vir = eps_vir.reshape(1, 128)
    return pl.pallas_call(
        kernel,
        out_shape=pltpu.VMEM((256, 1024), F32),
        in_specs=[hbm, hbm, smem, smem, vmem, vmem, vmem, vmem, smem],
        out_specs=vmem,
        scratch_shapes=[
            pltpu.VMEM((128, 2048), F32),
            pltpu.VMEM((2048, 1024), F32),
            pltpu.VMEM((2048, 1024), BF16),
            pltpu.VMEM((2048, 1024), BF16),
            pltpu.VMEM((n, 8, 2, ROWS, 128), F32),
            pltpu.VMEM((n, 8, 2, ROWS, 128), F32),
            pltpu.VMEM((n, 2, 4, 2, ROWS, 2048), F32),
            pltpu.VMEM((2, 16 * ROWS, 2048), BF16),
            pltpu.VMEM((n, 2, 2, 2, 2, ROWS, 1024), F32),
            pltpu.VMEM((n, 2, 2, 2, ROWS, 512), F32),
            pltpu.VMEM((n, 4, 2, 2, ROWS, 512), F32),
            pltpu.VMEM((n, 2, 2, ROWS, 1024), F32),
            pltpu.VMEM((n, 2, ROWS, 1024), F32),
            pltpu.VMEM((n, 16, ROWS, 128), F32),
            pltpu.VMEM((n, 16, ROWS, 128), F32),
            pltpu.VMEM((max(1, len(EARLY)), 32, ROWS, 128), F32),
            pltpu.VMEM((max(1, len(EARLY)), 32, ROWS, 128), F32),
            pltpu.VMEM((256, 128), F32),
            pltpu.VMEM((128, 128), F32),
            dma((19,)),
            dma((n,)), dma((n,)),
            dma((n,)), dma((n, 9)),
            dma((n,)), dma((n, 2)),
            dma((n,)), dma((n, 2)), dma((n,)),
            dma((n,)), dma((n,)),
            dma((n,)), dma((n,)),
        ],
        compiler_params=pltpu.CompilerParams(
            collective_id=0, has_side_effects=True, vmem_limit_bytes=60 * 2**20
        ),
        cost_estimate=pl.CostEstimate(
            flops=3 * 2 * 1024 * 2048 * 1024, bytes_accessed=10 * 2**20, transcendentals=0
        ),
        name="ladder",
    )(
        amplitudes, integrals, amp_mask, int_mask, int_mask, pairs.T,
        eps_occ.reshape(1, 200), eps_vir, eps_vir,
    )


def solution(mesh):
    return jax.shard_map(
        on_device,
        mesh=mesh,
        in_specs=(P("col", "row"), P("row", "col"), P(), P(), P("row", None), P(), P()),
        out_specs=P("row", "col"),
        check_vma=False,
    )
```

```python
import functools

import jax
import jax.numpy as jnp
from jax import lax
from jax.experimental import pallas as pl
from jax.experimental.pallas import tpu as pltpu
from jax.sharding import PartitionSpec as P

MESH = pl.DeviceIdType.MESH
ROUNDS = 8
ROWS = 64 // ROUNDS
F32 = jnp.float32
BF16 = jnp.bfloat16
Y_FIRST = frozenset((0, 3, 5,))
EARLY = (5, 6, 7,)
ORDER = (
    ("P", 0), ("P", 1), ("P", 2), ("C", 0), ("C", 1), ("C", 2), ("P", 3), ("P", 4), ("G1", 0),
    ("G1", 1), ("G1", 2), ("G1", 3), ("C", 3), ("G2a", 0), ("G2a", 1), ("G2b", 0), ("G2a", 2),
    ("P", 5), ("G2b", 1), ("G2a", 3), ("G3a", 0), ("G2b", 2), ("G1", 4), ("G2b", 3), ("G3a", 1),
    ("G3a", 2), ("P", 6), ("MA", 0), ("G3b", 0), ("MA", 1), ("G3b", 1), ("G3a", 3), ("MA", 2),
    ("G3b", 2), ("G1", 5), ("X1A", 0), ("G4", 0), ("G3b", 3), ("P", 7), ("G2a", 4), ("MA", 3),
    ("G2b", 4), ("X1A", 1), ("G4", 1), ("MB", 0), ("G1", 6), ("G4", 2), ("G4", 3), ("G2a", 5),
    ("X1A", 2), ("MB", 1), ("MB", 2), ("G2b", 5), ("X1B", 0), ("G3a", 4), ("X1A", 3), ("XA", 0),
    ("G3b", 4), ("G1", 7), ("MB", 3), ("G3a", 5), ("G2a", 6), ("G2b", 6), ("MA", 4), ("G4", 4),
    ("X1B", 1), ("MA", 5), ("XB", 0), ("G3b", 5), ("G2b", 7), ("MB", 4), ("G3a", 6), ("X1A", 4),
    ("G3b", 6), ("G2a", 7), ("XA", 1), ("XB", 1), ("X1B", 2), ("XA", 2), ("G4", 5), ("XA", 3),
    ("X1B", 3), ("MA", 6), ("X1A", 5), ("G3b", 7), ("ZA", 0), ("ZA", 1), ("G4", 6), ("MB", 5),
    ("G3a", 7), ("XB", 2), ("ZA", 2), ("ZB", 0), ("X1B", 4), ("XA", 4), ("MB", 6), ("XB", 3),
    ("G4", 7), ("X1A", 6), ("XA", 5), ("MA", 7), ("X1B", 5), ("ZB", 1), ("XB", 4), ("ZB", 2),
    ("MB", 7), ("ZA", 3), ("ZB", 3), ("F", 0), ("ZA", 4), ("X1B", 6), ("XA", 6), ("X1A", 7),
    ("XB", 5), ("X1B", 7), ("ZB", 4), ("ZA", 5), ("XB", 6), ("F", 1), ("F", 2), ("XA", 7),
    ("XB", 7), ("ZB", 5), ("ZA", 6), ("ZB", 6), ("F", 3), ("F", 4), ("F", 5), ("F", 6), ("ZA", 7),
    ("ZB", 7), ("F", 7),
)


def swap_bits(tiles, tile_bit, lane_bit):
    step = 1 << lane_bit
    lane = lax.broadcasted_iota(jnp.int32, tiles[0].shape, len(tiles[0].shape) - 1)
    upper = (lane & step) != 0
    result = list(tiles)
    for low in range(len(tiles)):
        if low >> tile_bit & 1:
            continue
        high = low | 1 << tile_bit
        a, b = tiles[low], tiles[high]
        result[low] = jnp.where(upper, pltpu.roll(b, step, 1), a)
        result[high] = jnp.where(upper, b, pltpu.roll(a, 128 - step, 1))
    return result


def split(value):
    hi = value.astype(BF16)
    return hi, (value - hi.astype(F32)).astype(BF16)


def kernel(
    t_hbm, v_hbm, am_s, im_s, im_v, pairs_v, eocc_v, evir_v, evir_s,
    out,
    tbuf, vbuf, vhi, vlo, pre_s, pre_r, slab, terms, part, xa, xf, zb, zr, post_s, post_r, twin_s, twin_r, occ, imf,
    load_sem, pre_ss, pre_rs, g_ss, g_rs, c_ss, c_rs, x_ss, xa_rs, xf_rs, z_ss, z_rs, o_ss, o_rs,
):
    row = lax.axis_index("row")
    col = lax.axis_index("col")
    zlo, x = row // 4, lax.rem(row, 4)
    y, zhi, core = col // 4, lax.rem(col // 2, 2), lax.rem(col, 2)
    chip = col // 2
    row_z = lax.rem(row + 4, 8)
    col_far = lax.rem(col + 8, 16)
    up = lax.rem(y + 1, 4)
    down = lax.rem(y + 3, 4)
    opposite = lax.rem(y + 2, 4)
    flip = 1 - zhi

    def col_of(yy, zz):
        return yy * 4 + zz * 2 + core

    dev_up = (row, col_of(up, zhi))
    dev_down = (row, col_of(down, zhi))
    dev_z = (row, col_of(y, flip))
    dev_core = (row, chip * 2 + 1 - core)
    dev_zlo = (row_z, col)
    right, left, across = lax.rem(x + 1, 4), lax.rem(x + 3, 4), lax.rem(x + 2, 4)
    dev_right = (zlo * 4 + right, col)
    dev_left = (zlo * 4 + left, col)
    own_off = 64 * (y // 2)
    send_off = 64 - own_off

    barrier = pltpu.get_barrier_semaphore()
    peers = [(r, col_far) for r in range(8)]
    peers += [(row, lax.rem(col + j, 16)) for j in range(1, 16)]
    peers += [dev_right, dev_left]
    peers += [(row_z, lax.rem(col + j, 16)) for j in range(16) if j != 8]
    for peer in peers:
        pl.semaphore_signal(barrier, inc=1, device_id=peer, device_id_type=MESH)

    def t_load(offset, count, which):
        rows = pl.ds(pl.multiple_of(offset, 8), count)
        return pltpu.make_async_copy(t_hbm.at[rows], tbuf.at[rows], load_sem.at[which])

    t_first = t_load(send_off, 2 * ROWS, 16)
    t_rest = t_load(send_off + 2 * ROWS, 64 - 2 * ROWS, 17)
    t_own = t_load(own_off, 64, 18)
    for load in (t_first, t_rest, t_own):
        load.start()

    def v_load(block):
        rows = pl.ds(block * 128, 128)
        return pltpu.make_async_copy(v_hbm.at[rows], vbuf.at[rows], load_sem.at[block])

    for block in range(16):
        v_load(block).start()

    def remote(src, dst, send_sem, recv_sem, device):
        return pltpu.make_async_remote_copy(
            src_ref=src, dst_ref=dst, send_sem=send_sem, recv_sem=recv_sem,
            device_id=device, device_id_type=MESH,
        )

    def drain(ref, sem):
        pltpu.make_async_copy(ref, ref, sem).wait()


    def masked_tile(offset, q, j):
        rows = pl.ds(pl.multiple_of(offset + q * ROWS, 8), ROWS)
        return tbuf[rows, j * 128 : (j + 1) * 128] * am_s[col, row * 16 + j].astype(F32)

    def pre_shuffle(q):
        tiles = [masked_tile(send_off, q, j) for j in range(16)]
        for bit in range(4):
            tiles = swap_bits(tiles, bit, bit)
        for bit in range(3):
            tiles = swap_bits(tiles, bit, bit + 4)
        for j in range(16):
            pre_s[q, j % 8, j // 8] = tiles[j]

    def pre_send(q):
        if q == 2:
            t_rest.wait()
        if q >= 2:
            pre_shuffle(q)
        for r in range(8):
            remote(
                pre_s.at[q, r], pre_r.at[q, row], pre_ss.at[q], pre_rs.at[q], (r, col_far)
            ).start()

    t_first.wait()
    pre_shuffle(0)
    pre_shuffle(1)
    pl.semaphore_wait(barrier, len(peers))

    def constants():
        imf[...] = im_v[...].astype(F32)

        ids = lax.broadcasted_iota(jnp.int32, (128, 128), 1)
        for block in range(2):
            rows = slice(block * 128, (block + 1) * 128)
            total = []
            for j in range(2):
                picked = jnp.transpose(jnp.broadcast_to(pairs_v[j : j + 1, rows], (128, 128)))
                total.append(
                    jnp.sum(jnp.where(picked == ids, eocc_v[:, 0:128], 0.0), axis=1, keepdims=True)
                    + jnp.sum(
                        jnp.where(picked[:, 0:72] == ids[:, 0:72] + 128, eocc_v[:, 128:200], 0.0),
                        axis=1, keepdims=True,
                    )
                )
            occ[rows, :] = jnp.broadcast_to(total[0] + total[1], (128, 128))

    def convert(block, _):
        v_load(block).wait()
        rows = pl.ds(pl.multiple_of(block * 128, 128), 128)
        for al in range(8):
            lanes = slice(al * 128, (al + 1) * 128)
            weight = im_s[row * 16 + block, col * 8 + al].astype(F32)
            hi, lo = split(vbuf[rows, lanes] * imf[...] * weight)
            vhi[rows, lanes] = hi
            vlo[rows, lanes] = lo
        return 0

    def slot(q, yy, zz, lanes=None):
        ref = slab.at[q, core, yy, zz]
        return ref if lanes is None else ref.at[:, lanes]

    LOWER, UPPER = pl.ds(0, 1024), pl.ds(1024, 1024)

    def push(q, kind, yy, zz, device, lanes=None):
        ref = slot(q, yy, zz, lanes)
        remote(ref, ref, g_ss.at[q], g_rs.at[q, kind], device).start()

    def arrived(q, kind, yy, zz, lanes=None):
        drain(slot(q, yy, zz, lanes), g_rs.at[q, kind])

    def to_core(q, yy, zz):
        ref = slot(q, yy, zz)
        half = 0 if zz is zhi else 1
        remote(ref, ref, c_ss.at[q], c_rs.at[q, half], dev_core).start()

    def g1(q):
        if q == 0:
            t_own.wait()
        drain(pre_r.at[q], pre_rs.at[q])
        tiles = [pre_r[q, j % 8, j // 8] for j in range(16)]
        for bit in range(3):
            tiles = swap_bits(tiles, bit, bit + 4)
        for j in range(16):
            slab[q, core, y, zhi, :, j * 128 : (j + 1) * 128] = masked_tile(own_off, q, j) + tiles[j]
        push(q, 1, y, zhi, dev_up)
        push(q, 2, y, zhi, dev_down)
        push(q, 0, y, zhi, dev_z)
        to_core(q, y, zhi)

    def g2a(q):
        arrived(q, 1, down, zhi)
        push(q, 3, down, zhi, dev_up, LOWER)
        arrived(q, 2, up, zhi)
        push(q, 4, up, zhi, dev_down, UPPER)
        if q in Y_FIRST:
            push(q, 5, down, zhi, dev_z)
            push(q, 6, up, zhi, dev_z)
        to_core(q, down, zhi)
        to_core(q, up, zhi)

    def g2b(q):
        arrived(q, 0, y, flip)
        if q not in Y_FIRST:
            push(q, 5, y, flip, dev_up)
            push(q, 6, y, flip, dev_down)
        to_core(q, y, flip)

    def g3a(q):
        arrived(q, 3, opposite, zhi, LOWER)
        arrived(q, 4, opposite, zhi, UPPER)
        if q in Y_FIRST:
            push(q, 7, opposite, zhi, dev_z)
        to_core(q, opposite, zhi)

    def g3b(q):
        arrived(q, 5, down, flip)
        if q not in Y_FIRST:
            push(q, 7, down, flip, dev_up, LOWER)
        arrived(q, 6, up, flip)
        if q not in Y_FIRST:
            push(q, 8, up, flip, dev_down, UPPER)
        to_core(q, down, flip)
        to_core(q, up, flip)

    def g4(q):
        if q in Y_FIRST:
            arrived(q, 7, opposite, flip)
        else:
            arrived(q, 7, opposite, flip, LOWER)
            arrived(q, 8, opposite, flip, UPPER)
        to_core(q, opposite, flip)

    parity = lax.rem(x, 2)

    def mm(q, plane, half):
        drain(slab.at[q, 0, pl.ds(0, 2)], c_rs.at[q, half])
        for k in range(2):
            for yy in range(0, 4, 2):
                value = jnp.concatenate([slab[q, k, yy, plane], slab[q, k, yy + 1, plane]], axis=0)
                hi, lo = split(value)
                at = (k * 4 + yy) * ROWS
                terms[half, at : at + 16, :] = hi
                terms[half, 64 + at : 80 + at, :] = lo
        for n in range(2):
            lanes = slice(n * 512, (n + 1) * 512)
            dot = functools.partial(jnp.dot, preferred_element_type=F32)
            both = dot(terms[half], vhi[:, lanes])
            acc = (both[:64] + both[64:]) + dot(terms[half, :64], vlo[:, lanes])
            part[q, plane, :, :, :, :, lanes] = acc.reshape(2, 2, 2, ROWS, 512)
            onward, back = (dev_right, dev_left) if n == 0 else (dev_left, dev_right)
            near = left if n == 0 else right

            @pl.when(parity == plane)
            def _():
                remote(
                    part.at[q, plane, :, :, across // 2, :, lanes], xa.at[q, n], x_ss.at[q],
                    xa_rs.at[q, n], onward,
                ).start()

            @pl.when(parity != plane)
            def _():
                remote(
                    part.at[q, plane, :, :, near // 2, :, lanes], xf.at[q, n], x_ss.at[q],
                    xf_rs.at[q], back,
                ).start()

    def join(q, plane):
        @pl.when(parity != plane)
        def _():
            for n in range(2):
                lanes = slice(n * 512, (n + 1) * 512)
                onward, near = (dev_right, right) if n == 0 else (dev_left, left)
                drain(xa.at[q, n], xa_rs.at[q, n])
                for k in range(2):
                    for z in range(2):
                        xa[q, n, k, z] = xa[q, n, k, z] + part[q, plane, k, z, near // 2, :, lanes]
                remote(xa.at[q, n], xf.at[q, 2 + n], x_ss.at[q], xf_rs.at[q], onward).start()

    def spread(tiles):
        for bit in range(3):
            tiles = swap_bits(tiles, bit, bit)
        for bit in range(3):
            tiles = swap_bits(tiles, bit, bit + 3)
        return swap_bits(tiles, 3, 6)

    def total(q, plane):
        @pl.when(parity == plane)
        def _():
            drain(xf.at[q], xf_rs.at[q])
            for side in (1, 0):
                z = lax.rem(zlo + side, 2)
                for k in range(2):
                    for n in range(2):
                        lanes = slice(n * 512, (n + 1) * 512)
                        zb[q, side, k, :, lanes] = (
                            part[q, plane, k, z, x // 2, :, lanes] + xf[q, n, k, z]
                        ) + xf[q, 2 + n, k, z]
                if side:
                    remote(zb.at[q, 1], zr.at[q], z_ss.at[q], z_rs.at[q], dev_zlo).start()
            if q in EARLY:
                e = EARLY.index(q)
                for side, there in ((0, row_z), (1, row)):
                    tiles = spread([
                        zb[q, side, k, :, al * 128 : (al + 1) * 128]
                        for k in range(2) for al in range(8)
                    ])
                    for c in range(16):
                        twin_s[e, side * 16 + c] = tiles[c]
                    for c in range(16):
                        copy = remote(
                            twin_s.at[e, side * 16 + c], twin_r.at[e, side * 16 + col],
                            o_ss.at[q], o_rs.at[q], (there, c),
                        )
                        if side:
                            pl.when(c != col)(copy.start)
                        else:
                            copy.start()
                twin_r[e, 16 + col] = twin_s[e, 16 + col]

    def out_rows(k, z, q):
        return pl.ds(pl.multiple_of(k * 128 + 64 * z + q * ROWS, 8), ROWS)

    def denominator(k, z, q, al):
        return (evir_s[0, col * 8 + al] + evir_v[...]) - occ[out_rows(k, z, q), :]

    def finish(q, plane):
        @pl.when(parity == plane)
        def _():
            drain(zr.at[q], z_rs.at[q])
            tiles = []
            for k in range(2):
                for al in range(8):
                    lanes = slice(al * 128, (al + 1) * 128)
                    value = zb[q, 0, k, :, lanes] + zr[q, k, :, lanes]
                    value = value / denominator(k, zlo, q, al)
                    out[out_rows(k, zlo, q), lanes] = value
                    tiles.append(value)
            if q not in EARLY:
                tiles = spread(tiles)
                for c in range(16):
                    post_s[q, c] = tiles[c]
                for c in range(16):
                    remote(
                        post_s.at[q, c], post_r.at[q, col], o_ss.at[q], o_rs.at[q], (row_z, c)
                    ).start()

    def fin(q):
        if q in EARLY:
            e = EARLY.index(q)
            drain(twin_r.at[e, pl.ds(0, 31)], o_rs.at[q])
            tiles = [twin_r[e, c] + twin_r[e, 16 + c] for c in range(16)]
        else:
            drain(post_r.at[q], o_rs.at[q])
            tiles = [post_r[q, c] for c in range(16)]
        for bit in range(3):
            tiles = swap_bits(tiles, bit, bit + 3)
        tiles = swap_bits(tiles, 3, 6)
        for k in range(2):
            for bl in range(8):
                value = tiles[k * 8 + bl]
                if q in EARLY:
                    value = value / denominator(k, 1 - zlo, q, bl)
                out[out_rows(k, 1 - zlo, q), bl * 128 : (bl + 1) * 128] = value

    def convert_four(i):
        if i == 0:
            constants()
        lax.fori_loop(4 * i, 4 * i + 4, convert, 0)

    stages = {
        "P": pre_send, "C": convert_four, "G1": g1, "G2a": g2a, "G2b": g2b, "G3a": g3a,
        "G3b": g3b, "G4": g4, "F": fin,
        "MA": lambda q: mm(q, zhi, 0), "MB": lambda q: mm(q, flip, 1),
        "X1A": lambda q: join(q, zhi), "X1B": lambda q: join(q, flip),
        "XA": lambda q: total(q, zhi), "XB": lambda q: total(q, flip),
        "ZA": lambda q: finish(q, zhi), "ZB": lambda q: finish(q, flip),
    }
    for stage, q in ORDER:
        stages[stage](q)

    for q in range(ROUNDS):
        drain(pre_s.at[q], pre_ss.at[q])
        drain(vbuf.at[pl.ds(0, 112)], g_ss.at[q])
        drain(slab.at[q, 0], c_ss.at[q])
        drain(vbuf.at[pl.ds(0, 96)], x_ss.at[q])
        drain(zr.at[q], z_ss.at[q])
        if q in EARLY:
            e = EARLY.index(q)
            drain(twin_s.at[e, pl.ds(0, 31)], o_ss.at[q])
        else:
            drain(post_s.at[q], o_ss.at[q])


def on_device(amplitudes, integrals, amp_mask, int_mask, pairs, eps_occ, eps_vir):
    vmem = pl.BlockSpec(memory_space=pltpu.VMEM)
    smem = pl.BlockSpec(memory_space=pltpu.SMEM)
    hbm = pl.BlockSpec(memory_space=pl.ANY)
    dma = pltpu.SemaphoreType.DMA
    n = ROUNDS
    eps_vir = eps_vir.reshape(1, 128)
    return pl.pallas_call(
        kernel,
        out_shape=pltpu.VMEM((256, 1024), F32),
        in_specs=[hbm, hbm, smem, smem, vmem, vmem, vmem, vmem, smem],
        out_specs=vmem,
        scratch_shapes=[
            pltpu.VMEM((128, 2048), F32),
            pltpu.VMEM((2048, 1024), F32),
            pltpu.VMEM((2048, 1024), BF16),
            pltpu.VMEM((2048, 1024), BF16),
            pltpu.VMEM((n, 8, 2, ROWS, 128), F32),
            pltpu.VMEM((n, 8, 2, ROWS, 128), F32),
            pltpu.VMEM((n, 2, 4, 2, ROWS, 2048), F32),
            pltpu.VMEM((2, 16 * ROWS, 2048), BF16),
            pltpu.VMEM((n, 2, 2, 2, 2, ROWS, 1024), F32),
            pltpu.VMEM((n, 2, 2, 2, ROWS, 512), F32),
            pltpu.VMEM((n, 4, 2, 2, ROWS, 512), F32),
            pltpu.VMEM((n, 2, 2, ROWS, 1024), F32),
            pltpu.VMEM((n, 2, ROWS, 1024), F32),
            pltpu.VMEM((n, 16, ROWS, 128), F32),
            pltpu.VMEM((n, 16, ROWS, 128), F32),
            pltpu.VMEM((max(1, len(EARLY)), 32, ROWS, 128), F32),
            pltpu.VMEM((max(1, len(EARLY)), 32, ROWS, 128), F32),
            pltpu.VMEM((256, 128), F32),
            pltpu.VMEM((128, 128), F32),
            dma((19,)),
            dma((n,)), dma((n,)),
            dma((n,)), dma((n, 9)),
            dma((n,)), dma((n, 2)),
            dma((n,)), dma((n, 2)), dma((n,)),
            dma((n,)), dma((n,)),
            dma((n,)), dma((n,)),
        ],
        compiler_params=pltpu.CompilerParams(
            collective_id=0, has_side_effects=True, vmem_limit_bytes=60 * 2**20
        ),
        cost_estimate=pl.CostEstimate(
            flops=3 * 2 * 1024 * 2048 * 1024, bytes_accessed=10 * 2**20, transcendentals=0
        ),
        name="ladder",
    )(
        amplitudes, integrals, amp_mask, int_mask, int_mask, pairs.T,
        eps_occ.reshape(1, 200), eps_vir, eps_vir,
    )


def solution(mesh):
    return jax.shard_map(
        on_device,
        mesh=mesh,
        in_specs=(P("col", "row"), P("row", "col"), P(), P(), P("row", None), P(), P()),
        out_specs=P("row", "col"),
        check_vma=False,
    )
```

```python
import functools

import jax
import jax.numpy as jnp
from jax import lax
from jax.experimental import pallas as pl
from jax.experimental.pallas import tpu as pltpu
from jax.sharding import PartitionSpec as P

MESH = pl.DeviceIdType.MESH
ROUNDS = 8
ROWS = 64 // ROUNDS
F32 = jnp.float32
BF16 = jnp.bfloat16
Y_FIRST = frozenset((0, 3, 5,))
EARLY = (5, 6, 7,)
ORDER = (
    ("P", 0), ("P", 1), ("P", 2), ("C", 0), ("C", 1), ("C", 2), ("P", 3), ("P", 4), ("G1", 0),
    ("G1", 1), ("G1", 2), ("G1", 3), ("C", 3), ("G2a", 0), ("G2a", 1), ("G2b", 0), ("G2a", 2),
    ("P", 5), ("G2b", 1), ("G2a", 3), ("G3a", 0), ("G2b", 2), ("G1", 4), ("G2b", 3), ("G3a", 1),
    ("G3a", 2), ("P", 6), ("MA", 0), ("G3b", 0), ("MA", 1), ("G3b", 1), ("G3a", 3), ("MA", 2),
    ("G3b", 2), ("G1", 5), ("X1A", 0), ("G4", 0), ("G3b", 3), ("P", 7), ("G2a", 4), ("MA", 3),
    ("G2b", 4), ("X1A", 1), ("G4", 1), ("MB", 0), ("G1", 6), ("G4", 2), ("G4", 3), ("G2a", 5),
    ("X1A", 2), ("MB", 1), ("MB", 2), ("G2b", 5), ("X1B", 0), ("G3a", 4), ("X1A", 3), ("XA", 0),
    ("G3b", 4), ("G1", 7), ("MB", 3), ("G3a", 5), ("G2a", 6), ("G2b", 6), ("MA", 4), ("G4", 4),
    ("X1B", 1), ("MA", 5), ("XB", 0), ("G3b", 5), ("G2b", 7), ("MB", 4), ("G3a", 6), ("X1A", 4),
    ("G3b", 6), ("G2a", 7), ("XA", 1), ("XB", 1), ("X1B", 2), ("XA", 2), ("G4", 5), ("XA", 3),
    ("X1B", 3), ("MA", 6), ("X1A", 5), ("G3b", 7), ("ZA", 0), ("ZA", 1), ("G4", 6), ("MB", 5),
    ("G3a", 7), ("XB", 2), ("ZA", 2), ("ZB", 0), ("X1B", 4), ("XA", 4), ("MB", 6), ("XB", 3),
    ("G4", 7), ("X1A", 6), ("XA", 5), ("MA", 7), ("X1B", 5), ("ZB", 1), ("XB", 4), ("ZB", 2),
    ("MB", 7), ("ZA", 3), ("ZB", 3), ("F", 0), ("ZA", 4), ("X1B", 6), ("XA", 6), ("X1A", 7),
    ("XB", 5), ("X1B", 7), ("ZB", 4), ("ZA", 5), ("XB", 6), ("F", 1), ("F", 2), ("XA", 7),
    ("XB", 7), ("ZB", 5), ("ZA", 6), ("ZB", 6), ("F", 3), ("F", 4), ("F", 5), ("F", 6), ("ZA", 7),
    ("ZB", 7), ("F", 7),
)


def swap_bits(tiles, tile_bit, lane_bit):
    step = 1 << lane_bit
    lane = lax.broadcasted_iota(jnp.int32, tiles[0].shape, len(tiles[0].shape) - 1)
    upper = (lane & step) != 0
    result = list(tiles)
    for low in range(len(tiles)):
        if low >> tile_bit & 1:
            continue
        high = low | 1 << tile_bit
        a, b = tiles[low], tiles[high]
        result[low] = jnp.where(upper, pltpu.roll(b, step, 1), a)
        result[high] = jnp.where(upper, b, pltpu.roll(a, 128 - step, 1))
    return result


def split(value):
    hi = value.astype(BF16)
    return hi, (value - hi.astype(F32)).astype(BF16)


def kernel(
    t_hbm, v_hbm, am_s, im_s, im_v, pairs_v, eocc_v, evir_v, evir_s,
    out,
    tbuf, vbuf, vhi, vlo, pre_s, pre_r, slab, terms, part, xa, xf, zb, zr, post_s, post_r, twin_s, twin_r, occ, imf,
    load_sem, pre_ss, pre_rs, g_ss, g_rs, c_ss, c_rs, x_ss, xa_rs, xf_rs, z_ss, z_rs, o_ss, o_rs,
):
    row = lax.axis_index("row")
    col = lax.axis_index("col")
    zlo, x = row // 4, lax.rem(row, 4)
    y, zhi, core = col // 4, lax.rem(col // 2, 2), lax.rem(col, 2)
    chip = col // 2
    row_z = lax.rem(row + 4, 8)
    col_far = lax.rem(col + 8, 16)
    up = lax.rem(y + 1, 4)
    down = lax.rem(y + 3, 4)
    opposite = lax.rem(y + 2, 4)
    flip = 1 - zhi

    def col_of(yy, zz):
        return yy * 4 + zz * 2 + core

    dev_up = (row, col_of(up, zhi))
    dev_down = (row, col_of(down, zhi))
    dev_z = (row, col_of(y, flip))
    dev_core = (row, chip * 2 + 1 - core)
    dev_zlo = (row_z, col)
    right, left, across = lax.rem(x + 1, 4), lax.rem(x + 3, 4), lax.rem(x + 2, 4)
    dev_right = (zlo * 4 + right, col)
    dev_left = (zlo * 4 + left, col)
    own_off = 64 * (y // 2)
    send_off = 64 - own_off

    def t_load(offset, count, which):
        rows = pl.ds(pl.multiple_of(offset, 8), count)
        return pltpu.make_async_copy(t_hbm.at[rows], tbuf.at[rows], load_sem.at[which])

    t_first = t_load(send_off, 2 * ROWS, 16)
    t_rest = t_load(send_off + 2 * ROWS, 64 - 2 * ROWS, 17)
    t_own = t_load(own_off, 64, 18)
    for load in (t_first, t_rest, t_own):
        load.start()

    barrier = pltpu.get_barrier_semaphore()
    peers = [(r, col_far) for r in range(8)]
    peers += [(row, lax.rem(col + j, 16)) for j in range(1, 16)]
    peers += [dev_right, dev_left]
    peers += [(row_z, lax.rem(col + j, 16)) for j in range(16) if j != 8]
    for peer in peers:
        pl.semaphore_signal(barrier, inc=1, device_id=peer, device_id_type=MESH)

    def v_load(block):
        rows = pl.ds(block * 128, 128)
        return pltpu.make_async_copy(v_hbm.at[rows], vbuf.at[rows], load_sem.at[block])

    for block in range(16):
        v_load(block).start()

    def remote(src, dst, send_sem, recv_sem, device):
        return pltpu.make_async_remote_copy(
            src_ref=src, dst_ref=dst, send_sem=send_sem, recv_sem=recv_sem,
            device_id=device, device_id_type=MESH,
        )

    def drain(ref, sem):
        pltpu.make_async_copy(ref, ref, sem).wait()


    def masked_tile(offset, q, j):
        rows = pl.ds(pl.multiple_of(offset + q * ROWS, 8), ROWS)
        return tbuf[rows, j * 128 : (j + 1) * 128] * am_s[col, row * 16 + j].astype(F32)

    def pre_shuffle(q):
        tiles = [masked_tile(send_off, q, j) for j in range(16)]
        for bit in range(4):
            tiles = swap_bits(tiles, bit, bit)
        for bit in range(3):
            tiles = swap_bits(tiles, bit, bit + 4)
        for j in range(16):
            pre_s[q, j % 8, j // 8] = tiles[j]

    def pre_send(q):
        if q == 2:
            t_rest.wait()
        if q >= 1:
            pre_shuffle(q)
        for r in range(8):
            remote(
                pre_s.at[q, r], pre_r.at[q, row], pre_ss.at[q], pre_rs.at[q], (r, col_far)
            ).start()

    t_first.wait()
    pre_shuffle(0)
    pl.semaphore_wait(barrier, len(peers))

    def constants():
        imf[...] = im_v[...].astype(F32)

        ids = lax.broadcasted_iota(jnp.int32, (128, 128), 1)
        for block in range(2):
            rows = slice(block * 128, (block + 1) * 128)
            total = []
            for j in range(2):
                picked = jnp.transpose(jnp.broadcast_to(pairs_v[j : j + 1, rows], (128, 128)))
                total.append(
                    jnp.sum(jnp.where(picked == ids, eocc_v[:, 0:128], 0.0), axis=1, keepdims=True)
                    + jnp.sum(
                        jnp.where(picked[:, 0:72] == ids[:, 0:72] + 128, eocc_v[:, 128:200], 0.0),
                        axis=1, keepdims=True,
                    )
                )
            occ[rows, :] = jnp.broadcast_to(total[0] + total[1], (128, 128))

    def convert(block, _):
        v_load(block).wait()
        rows = pl.ds(pl.multiple_of(block * 128, 128), 128)
        for al in range(8):
            lanes = slice(al * 128, (al + 1) * 128)
            weight = im_s[row * 16 + block, col * 8 + al].astype(F32)
            hi, lo = split(vbuf[rows, lanes] * imf[...] * weight)
            vhi[rows, lanes] = hi
            vlo[rows, lanes] = lo
        return 0

    def slot(q, yy, zz, lanes=None):
        ref = slab.at[q, core, yy, zz]
        return ref if lanes is None else ref.at[:, lanes]

    LOWER, UPPER = pl.ds(0, 1024), pl.ds(1024, 1024)

    def push(q, kind, yy, zz, device, lanes=None):
        ref = slot(q, yy, zz, lanes)
        remote(ref, ref, g_ss.at[q], g_rs.at[q, kind], device).start()

    def arrived(q, kind, yy, zz, lanes=None):
        drain(slot(q, yy, zz, lanes), g_rs.at[q, kind])

    def to_core(q, yy, zz):
        ref = slot(q, yy, zz)
        half = 0 if zz is zhi else 1
        remote(ref, ref, c_ss.at[q], c_rs.at[q, half], dev_core).start()

    def g1(q):
        if q == 0:
            t_own.wait()
        drain(pre_r.at[q], pre_rs.at[q])
        tiles = [pre_r[q, j % 8, j // 8] for j in range(16)]
        for bit in range(3):
            tiles = swap_bits(tiles, bit, bit + 4)
        for j in range(16):
            slab[q, core, y, zhi, :, j * 128 : (j + 1) * 128] = masked_tile(own_off, q, j) + tiles[j]
        push(q, 1, y, zhi, dev_up)
        push(q, 2, y, zhi, dev_down)
        push(q, 0, y, zhi, dev_z)
        to_core(q, y, zhi)

    def g2a(q):
        arrived(q, 1, down, zhi)
        push(q, 3, down, zhi, dev_up, LOWER)
        arrived(q, 2, up, zhi)
        push(q, 4, up, zhi, dev_down, UPPER)
        if q in Y_FIRST:
            push(q, 5, down, zhi, dev_z)
            push(q, 6, up, zhi, dev_z)
        to_core(q, down, zhi)
        to_core(q, up, zhi)

    def g2b(q):
        arrived(q, 0, y, flip)
        if q not in Y_FIRST:
            push(q, 5, y, flip, dev_up)
            push(q, 6, y, flip, dev_down)
        to_core(q, y, flip)

    def g3a(q):
        arrived(q, 3, opposite, zhi, LOWER)
        arrived(q, 4, opposite, zhi, UPPER)
        if q in Y_FIRST:
            push(q, 7, opposite, zhi, dev_z)
        to_core(q, opposite, zhi)

    def g3b(q):
        arrived(q, 5, down, flip)
        if q not in Y_FIRST:
            push(q, 7, down, flip, dev_up, LOWER)
        arrived(q, 6, up, flip)
        if q not in Y_FIRST:
            push(q, 8, up, flip, dev_down, UPPER)
        to_core(q, down, flip)
        to_core(q, up, flip)

    def g4(q):
        if q in Y_FIRST:
            arrived(q, 7, opposite, flip)
        else:
            arrived(q, 7, opposite, flip, LOWER)
            arrived(q, 8, opposite, flip, UPPER)
        to_core(q, opposite, flip)

    parity = lax.rem(x, 2)

    def mm(q, plane, half):
        drain(slab.at[q, 0, pl.ds(0, 2)], c_rs.at[q, half])
        for k in range(2):
            for yy in range(0, 4, 2):
                value = jnp.concatenate([slab[q, k, yy, plane], slab[q, k, yy + 1, plane]], axis=0)
                hi, lo = split(value)
                at = (k * 4 + yy) * ROWS
                terms[half, at : at + 16, :] = hi
                terms[half, 64 + at : 80 + at, :] = lo
        for n in range(2):
            lanes = slice(n * 512, (n + 1) * 512)
            dot = functools.partial(jnp.dot, preferred_element_type=F32)
            both = dot(terms[half], vhi[:, lanes])
            acc = (both[:64] + both[64:]) + dot(terms[half, :64], vlo[:, lanes])
            part[q, plane, :, :, :, :, lanes] = acc.reshape(2, 2, 2, ROWS, 512)
            onward, back = (dev_right, dev_left) if n == 0 else (dev_left, dev_right)
            near = left if n == 0 else right

            @pl.when(parity == plane)
            def _():
                remote(
                    part.at[q, plane, :, :, across // 2, :, lanes], xa.at[q, n], x_ss.at[q],
                    xa_rs.at[q, n], onward,
                ).start()

            @pl.when(parity != plane)
            def _():
                remote(
                    part.at[q, plane, :, :, near // 2, :, lanes], xf.at[q, n], x_ss.at[q],
                    xf_rs.at[q], back,
                ).start()

    def join(q, plane):
        @pl.when(parity != plane)
        def _():
            for n in range(2):
                lanes = slice(n * 512, (n + 1) * 512)
                onward, near = (dev_right, right) if n == 0 else (dev_left, left)
                drain(xa.at[q, n], xa_rs.at[q, n])
                for k in range(2):
                    for z in range(2):
                        xa[q, n, k, z] = xa[q, n, k, z] + part[q, plane, k, z, near // 2, :, lanes]
                remote(xa.at[q, n], xf.at[q, 2 + n], x_ss.at[q], xf_rs.at[q], onward).start()

    def spread(tiles):
        for bit in range(3):
            tiles = swap_bits(tiles, bit, bit)
        for bit in range(3):
            tiles = swap_bits(tiles, bit, bit + 3)
        return swap_bits(tiles, 3, 6)

    def total(q, plane):
        @pl.when(parity == plane)
        def _():
            drain(xf.at[q], xf_rs.at[q])
            for side in (1, 0):
                z = lax.rem(zlo + side, 2)
                for k in range(2):
                    for n in range(2):
                        lanes = slice(n * 512, (n + 1) * 512)
                        zb[q, side, k, :, lanes] = (
                            part[q, plane, k, z, x // 2, :, lanes] + xf[q, n, k, z]
                        ) + xf[q, 2 + n, k, z]
                if side:
                    remote(zb.at[q, 1], zr.at[q], z_ss.at[q], z_rs.at[q], dev_zlo).start()
            if q in EARLY:
                e = EARLY.index(q)
                for side, there in ((0, row_z), (1, row)):
                    tiles = spread([
                        zb[q, side, k, :, al * 128 : (al + 1) * 128]
                        for k in range(2) for al in range(8)
                    ])
                    for c in range(16):
                        twin_s[e, side * 16 + c] = tiles[c]
                    for c in range(16):
                        copy = remote(
                            twin_s.at[e, side * 16 + c], twin_r.at[e, side * 16 + col],
                            o_ss.at[q], o_rs.at[q], (there, c),
                        )
                        if side:
                            pl.when(c != col)(copy.start)
                        else:
                            copy.start()
                twin_r[e, 16 + col] = twin_s[e, 16 + col]

    def out_rows(k, z, q):
        return pl.ds(pl.multiple_of(k * 128 + 64 * z + q * ROWS, 8), ROWS)

    def denominator(k, z, q, al):
        return (evir_s[0, col * 8 + al] + evir_v[...]) - occ[out_rows(k, z, q), :]

    def finish(q, plane):
        @pl.when(parity == plane)
        def _():
            drain(zr.at[q], z_rs.at[q])
            tiles = []
            for k in range(2):
                for al in range(8):
                    lanes = slice(al * 128, (al + 1) * 128)
                    value = zb[q, 0, k, :, lanes] + zr[q, k, :, lanes]
                    value = value / denominator(k, zlo, q, al)
                    out[out_rows(k, zlo, q), lanes] = value
                    tiles.append(value)
            if q not in EARLY:
                tiles = spread(tiles)
                for c in range(16):
                    post_s[q, c] = tiles[c]
                for c in range(16):
                    remote(
                        post_s.at[q, c], post_r.at[q, col], o_ss.at[q], o_rs.at[q], (row_z, c)
                    ).start()

    def fin(q):
        if q in EARLY:
            e = EARLY.index(q)
            drain(twin_r.at[e, pl.ds(0, 31)], o_rs.at[q])
            tiles = [twin_r[e, c] + twin_r[e, 16 + c] for c in range(16)]
        else:
            drain(post_r.at[q], o_rs.at[q])
            tiles = [post_r[q, c] for c in range(16)]
        for bit in range(3):
            tiles = swap_bits(tiles, bit, bit + 3)
        tiles = swap_bits(tiles, 3, 6)
        for k in range(2):
            for bl in range(8):
                value = tiles[k * 8 + bl]
                if q in EARLY:
                    value = value / denominator(k, 1 - zlo, q, bl)
                out[out_rows(k, 1 - zlo, q), bl * 128 : (bl + 1) * 128] = value

    def convert_four(i):
        if i == 0:
            constants()
        lax.fori_loop(4 * i, 4 * i + 4, convert, 0)

    stages = {
        "P": pre_send, "C": convert_four, "G1": g1, "G2a": g2a, "G2b": g2b, "G3a": g3a,
        "G3b": g3b, "G4": g4, "F": fin,
        "MA": lambda q: mm(q, zhi, 0), "MB": lambda q: mm(q, flip, 1),
        "X1A": lambda q: join(q, zhi), "X1B": lambda q: join(q, flip),
        "XA": lambda q: total(q, zhi), "XB": lambda q: total(q, flip),
        "ZA": lambda q: finish(q, zhi), "ZB": lambda q: finish(q, flip),
    }
    for stage, q in ORDER:
        stages[stage](q)

    for q in range(ROUNDS):
        drain(pre_s.at[q], pre_ss.at[q])
        drain(vbuf.at[pl.ds(0, 112)], g_ss.at[q])
        drain(slab.at[q, 0], c_ss.at[q])
        drain(vbuf.at[pl.ds(0, 96)], x_ss.at[q])
        drain(zr.at[q], z_ss.at[q])
        if q in EARLY:
            e = EARLY.index(q)
            drain(twin_s.at[e, pl.ds(0, 31)], o_ss.at[q])
        else:
            drain(post_s.at[q], o_ss.at[q])


def on_device(amplitudes, integrals, amp_mask, int_mask, pairs, eps_occ, eps_vir):
    vmem = pl.BlockSpec(memory_space=pltpu.VMEM)
    smem = pl.BlockSpec(memory_space=pltpu.SMEM)
    hbm = pl.BlockSpec(memory_space=pl.ANY)
    dma = pltpu.SemaphoreType.DMA
    n = ROUNDS
    eps_vir = eps_vir.reshape(1, 128)
    return pl.pallas_call(
        kernel,
        out_shape=pltpu.VMEM((256, 1024), F32),
        in_specs=[hbm, hbm, smem, smem, vmem, vmem, vmem, vmem, smem],
        out_specs=vmem,
        scratch_shapes=[
            pltpu.VMEM((128, 2048), F32),
            pltpu.VMEM((2048, 1024), F32),
            pltpu.VMEM((2048, 1024), BF16),
            pltpu.VMEM((2048, 1024), BF16),
            pltpu.VMEM((n, 8, 2, ROWS, 128), F32),
            pltpu.VMEM((n, 8, 2, ROWS, 128), F32),
            pltpu.VMEM((n, 2, 4, 2, ROWS, 2048), F32),
            pltpu.VMEM((2, 16 * ROWS, 2048), BF16),
            pltpu.VMEM((n, 2, 2, 2, 2, ROWS, 1024), F32),
            pltpu.VMEM((n, 2, 2, 2, ROWS, 512), F32),
            pltpu.VMEM((n, 4, 2, 2, ROWS, 512), F32),
            pltpu.VMEM((n, 2, 2, ROWS, 1024), F32),
            pltpu.VMEM((n, 2, ROWS, 1024), F32),
            pltpu.VMEM((n, 16, ROWS, 128), F32),
            pltpu.VMEM((n, 16, ROWS, 128), F32),
            pltpu.VMEM((max(1, len(EARLY)), 32, ROWS, 128), F32),
            pltpu.VMEM((max(1, len(EARLY)), 32, ROWS, 128), F32),
            pltpu.VMEM((256, 128), F32),
            pltpu.VMEM((128, 128), F32),
            dma((19,)),
            dma((n,)), dma((n,)),
            dma((n,)), dma((n, 9)),
            dma((n,)), dma((n, 2)),
            dma((n,)), dma((n, 2)), dma((n,)),
            dma((n,)), dma((n,)),
            dma((n,)), dma((n,)),
        ],
        compiler_params=pltpu.CompilerParams(
            collective_id=0, has_side_effects=True, vmem_limit_bytes=60 * 2**20
        ),
        cost_estimate=pl.CostEstimate(
            flops=3 * 2 * 1024 * 2048 * 1024, bytes_accessed=10 * 2**20, transcendentals=0
        ),
        name="ladder",
    )(
        amplitudes, integrals, amp_mask, int_mask, int_mask, pairs.T,
        eps_occ.reshape(1, 200), eps_vir, eps_vir,
    )


def solution(mesh):
    return jax.shard_map(
        on_device,
        mesh=mesh,
        in_specs=(P("col", "row"), P("row", "col"), P(), P(), P("row", None), P(), P()),
        out_specs=P("row", "col"),
        check_vma=False,
    )
```
